32 devices in a mesh: dp: 8 (over z, core), seq: 4 (over y, x).
Axes of the slice: x: 2, y: 2, z: 4, core: 2. Of those that a mesh axis runs over, the one named last changes fastest.
Arguments:
- tokens: bfloat16 [8, 2048, 1024], P('dp', 'seq'), may hold values from -6 to 6
- cotangent: bfloat16 [8, 2048, 1024], P('dp', 'seq'), may hold values from -6 to 6
- gain_mixer: bfloat16 [1024], P(('dp', 'seq')), may hold values from 0.25 to 1.75
- proj_input: bfloat16 [1024, 4096], P(('dp', 'seq')), may hold values from -0.1875 to 0.1875
- conv_filter: bfloat16 [4096, 4], P(('dp', 'seq')), may hold values from -3 to 3
- proj_gates: bfloat16 [1024, 16], P(('dp', 'seq')), may hold values from -0.1875 to 0.1875
- proj_outgate: bfloat16 [1024, 2048], P(('dp', 'seq')), may hold values from -0.1875 to 0.1875
- gain_heads: bfloat16 [256], P(('dp', 'seq')), may hold values from 0.25 to 1.75
- proj_output: bfloat16 [2048, 1024], P(('dp', 'seq')), may hold values from -0.1875 to 0.1875
- gain_feed: bfloat16 [1024], P(('dp', 'seq')), may hold values from 0.25 to 1.75
- feed_gate: bfloat16 [1024, 2816], P(('dp', 'seq')), may hold values from -0.1875 to 0.1875
- feed_up: bfloat16 [1024, 2816], P(('dp', 'seq')), may hold values from -0.1875 to 0.1875
- feed_down: bfloat16 [2816, 1024], P(('dp', 'seq')), may hold values from -0.109375 to 0.109375
- decay_log: float32 [8], replicated, may hold values from -7.8 to -3.2
- decay_bias: float32 [8], replicated, may hold values from -1 to 1
Outputs:
- layer_out: bfloat16 [8, 2048, 1024], P('dp', 'seq')
- tokens_grad: float32 [8, 2048, 1024], P('dp', 'seq')
- grad_gain_mixer: float32 [1024], P(('dp', 'seq'))
- grad_proj_input: float32 [1024, 4096], P(('dp', 'seq'))
- grad_conv_filter: float32 [4096, 4], P(('dp', 'seq'))
- grad_proj_gates: float32 [1024, 16], P(('dp', 'seq'))
- grad_proj_outgate: float32 [1024, 2048], P(('dp', 'seq'))
- grad_gain_heads: float32 [256], P(('dp', 'seq'))
- grad_proj_output: float32 [2048, 1024], P(('dp', 'seq'))
- grad_gain_feed: float32 [1024], P(('dp', 'seq'))
- grad_feed_gate: float32 [1024, 2816], P(('dp', 'seq'))
- grad_feed_up: float32 [1024, 2816], P(('dp', 'seq'))
- grad_feed_down: float32 [2816, 1024], P(('dp', 'seq'))
- grad_decay_log: float32 [8], replicated
- grad_decay_bias: float32 [8], replicated
The draws below stay inside these ranges and needn't reach their ends.
All inputs are finite; a program needn't handle non-finite values.
Results may differ from the reference program's by a relative error of at most 0.017.
Values may be sent and summed in bfloat16 or wider, within the bound.
No kernel may reach another device: no remote copies, remote signals or barrier semaphores. Data moves between devices by JAX's collectives and lax.ppermute only.
A program may use at most 320 MiB of HBM per device.

```python
from functools import partial
import jax
import jax.numpy as jnp
from jax import lax

D = 1024
HEADS = 8
DK = 128
DV = 256
FF = 2816
CONV = 4
SPAN = 64
LENGTH = 2048
BATCH = 8


def with_spikes(array, rng, source, target, shards_of, factor):
    owner, partner = [(jnp.arange(array.shape[position]) // (array.shape[position] // shards_of)).reshape([-1 if axis == position else 1 for axis in range(array.ndim)]) for position in (source, target)]
    chosen = jax.random.permutation(rng, shards_of)[partner]
    strong = (owner == chosen) | (owner == (partner + shards_of // 2) % shards_of)
    return jnp.where(strong, factor * array, array)


def block_levels(own_key, extent, cuts, low, high):
    factor_of, own = 1.0, jax.random.fold_in(own_key, 6)
    for dim, shards_of in cuts:
        steps = jnp.exp(jax.random.uniform(jax.random.fold_in(own, dim), (shards_of,), jnp.float32, low / len(cuts), high / len(cuts)))
        factor_of = factor_of * jnp.repeat(steps, extent[dim] // shards_of).reshape([-1 if axis == dim else 1 for axis in range(len(extent))])
    return factor_of


def bell_draw(stream_key, extent, deviation, limit, pieces=(), held_as=jnp.bfloat16):
    factor_of = block_levels(stream_key, extent, pieces, -0.22, 0.18) if pieces else 1.0
    entries = jax.random.normal(stream_key, extent, jnp.float32) * deviation * factor_of
    return jnp.minimum(jnp.maximum(entries, -limit), limit).astype(held_as)


def bell_draw_with(own_key, shape, spread, reach, split, heavy, dtype=jnp.bfloat16):
    values = spread * jax.random.normal(own_key, shape, jnp.float32)
    if split:
        values = values * block_levels(own_key, shape, split, -0.22, 0.18)
    return jnp.clip(with_spikes(values, jax.random.fold_in(own_key, 3), *heavy), -reach, reach).astype(dtype)


def setup_inputs(seed: int = 0) -> dict:
    seeds = jax.random.split(jax.random.key(seed), 16)
    return {
        "tokens": bell_draw(seeds[0], (BATCH, LENGTH, D), 1.0, 6.0, ((0, 8), (1, 4))),
        "cotangent": bell_draw_with(seeds[1], (BATCH, LENGTH, D), 1.0, 6.0, ((0, 8), (1, 4)), (0, 2, 8, 2.0)),
        "gain_mixer": jnp.clip(1.0 + 0.15 * jax.random.normal(seeds[2], (D,), jnp.float32), 0.25, 1.75).astype(jnp.bfloat16),
        "proj_input": bell_draw(seeds[3], (D, 2 * HEADS * DK + HEADS * DV), D ** -0.5, 0.1875, ((0, 32),)),
        "conv_filter": bell_draw(seeds[4], (2 * HEADS * DK + HEADS * DV, CONV), CONV ** -0.5, 3.0, ((0, 32),)),
        "proj_gates": bell_draw(seeds[5], (D, 2 * HEADS), D ** -0.5, 0.1875, ((0, 32),)),
        "proj_outgate": bell_draw(seeds[6], (D, HEADS * DV), D ** -0.5, 0.1875, ((0, 32),)),
        "gain_heads": jnp.clip(1.0 + 0.15 * jax.random.normal(seeds[7], (DV,), jnp.float32), 0.25, 1.75).astype(jnp.bfloat16),
        "proj_output": bell_draw(seeds[8], (HEADS * DV, D), D ** -0.5, 0.1875, ((0, 32),)),
        "gain_feed": jnp.clip(1.0 + 0.15 * jax.random.normal(seeds[9], (D,), jnp.float32), 0.25, 1.75).astype(jnp.bfloat16),
        "feed_gate": bell_draw(seeds[10], (D, FF), D ** -0.5, 0.1875, ((0, 32),)),
        "feed_up": bell_draw(seeds[11], (D, FF), D ** -0.5, 0.1875, ((0, 32),)),
        "feed_down": bell_draw(seeds[12], (FF, D), FF ** -0.5, 0.109375, ((0, 32),)),
        "decay_log": jnp.clip(jax.random.uniform(seeds[13], (HEADS,), jnp.float32, -7.8, -3.2), -7.8, -3.2),
        "decay_bias": jnp.clip(jax.random.uniform(seeds[14], (HEADS,), jnp.float32, -1.0, 1.0), -1.0, 1.0),
    }


@jax.custom_vjp
def low(v):
    return lax.optimization_barrier(v.astype(jnp.bfloat16)).astype(jnp.float32)

@jax.custom_vjp
def low_back(v):
    return v

def low_keep(v):
    return (low(v), None)

def low_pass(kept, grad):
    return (grad,)

def back_keep(v):
    return (v, None)

def back_low(kept, grad):
    return (low(grad),)
low.defvjp(low_keep, low_pass)
low_back.defvjp(back_keep, back_low)
HIGH = lax.Precision.HIGHEST
EPS = 1e-06

def matmul(left, right):
    return jnp.dot(left, right, precision=HIGH)

def silu(value):
    return value * jax.nn.sigmoid(value)

def rmsnorm(value, gain):
    return value * lax.rsqrt(lax.optimization_barrier(jnp.mean(value * value, axis=-1, keepdims=True)) + EPS) * gain

def unit_rows(value):
    return value * lax.rsqrt(lax.optimization_barrier(jnp.sum(value * value, axis=-1, keepdims=True)) + EPS)

def token_step(state, item):
    query, key, value, beta, decay = item
    along = jnp.einsum('hd,hde->he', key, state, precision=HIGH)
    erased = state - beta[:, None, None] * key[:, :, None] * along[:, None, :]
    state = jnp.exp(decay)[:, None, None] * erased + beta[:, None, None] * key[:, :, None] * value[:, None, :]
    return (state, jnp.einsum('hd,hde->he', query, state, precision=HIGH))

def rule_block(state, block):
    return lax.scan(token_step, state, block)

def delta_rule(queries, keys, values, betas, decays):
    length = keys.shape[0]

    def blocked(value):
        return value.reshape(length // SPAN, SPAN, *value.shape[1:])
    start = jnp.zeros((HEADS, DK, DV), jnp.float32)
    inputs = (blocked(queries), blocked(keys), blocked(values), blocked(betas), blocked(decays))
    _, outs = lax.scan(jax.checkpoint(rule_block), start, inputs)
    return outs.reshape(length, HEADS, DV)

def layer(sequence, params):
    gain_mixer, proj_input, conv_filter, proj_gates, proj_outgate, gain_heads, proj_output, gain_feed, feed_gate, feed_up, feed_down, decay_log, decay_bias = params
    length = sequence.shape[0]
    width = HEADS * DK
    first = low(rmsnorm(sequence, gain_mixer))
    projected = low_back(low(matmul(first, proj_input)))
    padded = jnp.concatenate([jnp.zeros((CONV - 1, projected.shape[1]), jnp.float32), projected], axis=0)
    convolved = conv_filter[:, 0] * padded[0:length]
    for offset in range(1, CONV):
        convolved = convolved + conv_filter[:, offset] * padded[offset:offset + length]
    activated = silu(convolved)
    queries = unit_rows(activated[:, :width].reshape(length, HEADS, DK)) * DK ** (-0.5)
    keys = unit_rows(activated[:, width:2 * width].reshape(length, HEADS, DK))
    values = activated[:, 2 * width:].reshape(length, HEADS, DV)
    gate_pre = low_back(matmul(first, proj_gates))
    betas = jax.nn.sigmoid(gate_pre[:, :HEADS])
    decays = -jnp.exp(decay_log) * jax.nn.softplus(gate_pre[:, HEADS:] + decay_bias)
    mixed = delta_rule(queries, keys, values, betas, decays)
    outgate = low_back(matmul(first, proj_outgate)).reshape(length, HEADS, DV)
    gated = low((rmsnorm(mixed, gain_heads) * silu(outgate)).reshape(length, HEADS * DV))
    middle = sequence + low_back(matmul(gated, proj_output))
    second = low(rmsnorm(middle, gain_feed))
    up_gate = low_back(matmul(second, feed_gate))
    up_linear = low_back(matmul(second, feed_up))
    hidden = low(silu(up_gate) * up_linear)
    return middle + low_back(matmul(hidden, feed_down))

def forward(tokens, params):
    return lax.map(jax.checkpoint(partial(layer, params=params)), tokens)

def reference(tokens, cotangent, gain_mixer, proj_input, conv_filter, proj_gates, proj_outgate, gain_heads, proj_output, gain_feed, feed_gate, feed_up, feed_down, decay_log, decay_bias):
    params = tuple((value.astype(jnp.float32) for value in (gain_mixer, proj_input, conv_filter, proj_gates, proj_outgate, gain_heads, proj_output, gain_feed, feed_gate, feed_up, feed_down, decay_log, decay_bias)))
    layer_out, pull = jax.vjp(forward, tokens.astype(jnp.float32), params)
    tokens_grad, grads = pull(cotangent.astype(jnp.float32))
    grad_gain_mixer, grad_proj_input, grad_conv_filter, grad_proj_gates, grad_proj_outgate, grad_gain_heads, grad_proj_output, grad_gain_feed, grad_feed_gate, grad_feed_up, grad_feed_down, grad_decay_log, grad_decay_bias = grads
    return (layer_out.astype(jnp.bfloat16), tokens_grad, grad_gain_mixer, grad_proj_input, grad_conv_filter, grad_proj_gates, grad_proj_outgate, grad_gain_heads, grad_proj_output, grad_gain_feed, grad_feed_gate, grad_feed_up, grad_feed_down, grad_decay_log, grad_decay_bias)
```

```python
import functools
import math
import jax
import jax.numpy as jnp
from jax import lax
from jax.experimental import pallas as pl
from jax.experimental.pallas import tpu as pltpu
from jax.sharding import PartitionSpec as P

D = 1024
HEADS = 8
DK = 128
DV = 256
CONV = 4
CHUNK = 128
PAIR = 2
EPS = 1e-06
WIDE = DV + DK
VMEM = 56 * 1024 * 1024
BF = jnp.bfloat16
F32 = jnp.float32


def mm(left, right, over=(1, 0)):
    return lax.dot_general(
        left.astype(BF), right.astype(BF), (((over[0],), (over[1],)), ((), ())), preferred_element_type=F32
    )


def mm_nt(left, right):
    return mm(left, right, (1, 1))


def mm_tn(left, right):
    return mm(left, right, (0, 0))


def grids():
    rows = lax.broadcasted_iota(jnp.int32, (CHUNK, CHUNK), 0)
    cols = lax.broadcasted_iota(jnp.int32, (CHUNK, CHUNK), 1)
    return rows, cols


def to_column(row, rows, cols):
    return jnp.sum(jnp.where(rows == cols, row, 0.0), axis=1, keepdims=True)


def to_row(column, rows, cols):
    return jnp.sum(jnp.where(rows == cols, column, 0.0), axis=0, keepdims=True)


def fades(decay_row, beta_row, rows, cols):
    cumul = jnp.sum(jnp.where(cols <= rows, decay_row, 0.0), axis=1, keepdims=True)
    cumul_row = to_row(cumul, rows, cols)
    beta = to_column(beta_row, rows, cols)
    fading = jnp.exp(jnp.minimum(cumul - cumul_row, 0.0))
    strict = jnp.where(rows > cols, fading, 0.0)
    causal = jnp.where(rows >= cols, fading, 0.0)
    last = cumul[CHUNK - 1 : CHUNK]
    return beta, strict, causal, jnp.exp(cumul), jnp.exp(last - cumul), jnp.exp(last)


def unit_lower_inverse(lower, rows, cols):
    def level(width):
        shift = width.bit_length() - 1
        row_block, col_block = lax.shift_right_logical(rows, shift), lax.shift_right_logical(cols, shift)
        return jnp.where((row_block == col_block + 1) & ((col_block & 1) == 0), lower, 0.0)

    inverse = jnp.where(rows == cols, 1.0, 0.0) - level(1)
    width = 2
    while width < CHUNK:
        inverse = inverse - mm(mm(inverse, level(width)), inverse)
        width *= 2
    return inverse


def convolve(x, edge, taps, held, piece):
    held[0:8] = edge
    held[8 : 8 + piece] = x.astype(F32)
    total = taps[0:1] * held[5 : 5 + piece]
    for j in range(1, CONV):
        total = total + taps[j : j + 1] * held[5 + j : 5 + j + piece]
    return total


def units(active):
    inverse = lax.rsqrt(jnp.sum(active * active, axis=-1, keepdims=True) + EPS)
    return active * inverse, inverse


def opening_kernel(
    piece, q_ref, k_ref, v_ref, qe_ref, ke_ref, ve_ref, qf_ref, kf_ref, vf_ref, beta_ref, decay_ref,
    local_ref, reading_ref, states_ref, inverse_ref, held_q, held_k, held_v,
):
    rows, cols = grids()
    q_conv = convolve(q_ref[...], qe_ref[...], qf_ref[...], held_q, piece)
    k_conv = convolve(k_ref[...], ke_ref[...], kf_ref[...], held_k, piece)
    v_conv = convolve(v_ref[...], ve_ref[...], vf_ref[...], held_v, piece)
    q_act = q_conv * jax.nn.sigmoid(q_conv)
    k_act = k_conv * jax.nn.sigmoid(k_conv)
    v_act = v_conv * jax.nn.sigmoid(v_conv)
    for head in range(PAIR):
        queries = units(q_act[:, head * DK : (head + 1) * DK])[0] * DK**-0.5
        keys = units(k_act[:, head * DK : (head + 1) * DK])[0]
        values = v_act[:, head * DV : (head + 1) * DV]
        state = jnp.concatenate(
            [jnp.zeros((DK, DV), F32), jnp.where(rows == cols, 1.0, 0.0)], axis=1
        )
        for chunk in range(piece // CHUNK):
            part = slice(chunk * CHUNK, (chunk + 1) * CHUNK)
            query, key, value = queries[part], keys[part], values[part]
            beta, strict, causal, grow, fade, closing = fades(
                decay_ref[head, :, part], beta_ref[head, :, part], rows, cols
            )
            both = mm_nt(jnp.concatenate([key, query], axis=0), key)
            inverse = unit_lower_inverse(beta * both[:CHUNK] * strict, rows, cols)
            scores = both[CHUNK:] * causal
            inverse_ref[part, head * CHUNK : (head + 1) * CHUNK] = inverse.astype(BF)
            seen = mm(jnp.concatenate([key * grow, query * grow], axis=0), state)
            wide = jnp.concatenate([value, jnp.zeros((CHUNK, DK), F32)], axis=1)
            fresh = mm(inverse, beta * (wide - seen[:CHUNK]))
            result = seen[CHUNK:] + mm(scores, fresh)
            state = closing * state + mm_tn(key * fade, fresh)
            local_ref[part, head * DV : (head + 1) * DV] = result[:, :DV]
            reading_ref[part, head * DK : (head + 1) * DK] = result[:, DV:].astype(BF)
            states_ref[0, head, chunk] = state.astype(BF)


def finish_kernel(local_ref, reading_ref, incoming_ref, outgate_ref, gain_ref, mixed_ref, gated_ref):
    for head in range(PAIR):
        wide = slice(head * DV, (head + 1) * DV)
        mixed = local_ref[:, wide] + mm(reading_ref[:, head * DK : (head + 1) * DK], incoming_ref[0, head])
        mixed_ref[:, wide] = mixed
        inverse = lax.rsqrt(jnp.mean(mixed * mixed, axis=-1, keepdims=True) + EPS)
        outgate = outgate_ref[:, wide]
        gated = mixed * inverse * gain_ref[0:1] * (outgate * jax.nn.sigmoid(outgate))
        gated_ref[:, wide] = gated.astype(BF)


def unfinish_kernel(
    grad_ref, mixed_ref, outgate_ref, gain_ref, reading_ref, grad_mixed_ref, grad_outgate_ref, gain_grad_ref, flow_ref
):
    gain = gain_ref[0:1]
    for head in range(PAIR):
        wide = slice(head * DV, (head + 1) * DV)
        mixed, outgate, grad = mixed_ref[:, wide], outgate_ref[:, wide], grad_ref[:, wide]
        inverse = lax.rsqrt(jnp.mean(mixed * mixed, axis=-1, keepdims=True) + EPS)
        normed = mixed * inverse
        sigmoid = jax.nn.sigmoid(outgate)
        gate = outgate * sigmoid
        along = grad * normed
        gain_grad = jnp.sum(along * gate, axis=0, keepdims=True)
        gain_grad_ref[0, head] = jnp.broadcast_to(gain_grad, (8, DV))
        grad_outgate_ref[:, wide] = (along * gain * (sigmoid + gate * (1.0 - sigmoid))).astype(BF)
        scaled = grad * gain * gate
        grad_mixed = inverse * (scaled - normed * jnp.mean(scaled * normed, axis=-1, keepdims=True))
        grad_mixed_ref[:, wide] = grad_mixed.astype(BF)
        flow_ref[0, head] = mm_tn(reading_ref[:, head * DK : (head + 1) * DK], grad_mixed)


def unconvolve(grad, taps, held_in, held_out, piece, grad_ref, edge_ref, taps_ref):
    width = grad.shape[1]
    held_out[0:8] = jnp.zeros((8, width), F32)
    held_out[8 : 8 + piece] = grad
    held_out[8 + piece : 16 + piece] = jnp.zeros((8, width), F32)
    total = taps[0:1] * held_out[11 : 11 + piece]
    edge = taps[0:1] * held_out[3:11]
    for j in range(1, CONV):
        total = total + taps[j : j + 1] * held_out[11 - j : 11 - j + piece]
        edge = edge + taps[j : j + 1] * held_out[3 - j : 11 - j]
    grad_ref[...] = total.astype(BF)
    edge_ref[...] = edge
    sums = [jnp.sum(grad * held_in[5 + j : 5 + j + piece], axis=0, keepdims=True) for j in range(CONV)]
    taps_ref[0] = jnp.concatenate(sums + [jnp.zeros((8 - CONV, width), F32)], axis=0)


def silu_slope(value, sigmoid):
    return sigmoid * (1.0 + value * (1.0 - sigmoid))


def closing_kernel(
    piece, q_ref, k_ref, v_ref, qe_ref, ke_ref, ve_ref, qf_ref, kf_ref, vf_ref, beta_ref, decay_ref,
    inverse_ref, states_ref, incoming_ref, grad_ref, leaving_ref,
    dq_ref, dk_ref, dv_ref, dqe_ref, dke_ref, dve_ref, dqf_ref, dkf_ref, dvf_ref, dbeta_ref, ddecay_ref,
    held_q, held_k, held_v, back_q, back_k, back_v,
):
    rows, cols = grids()
    q_conv = convolve(q_ref[...], qe_ref[...], qf_ref[...], held_q, piece)
    k_conv = convolve(k_ref[...], ke_ref[...], kf_ref[...], held_k, piece)
    v_conv = convolve(v_ref[...], ve_ref[...], vf_ref[...], held_v, piece)
    q_sig, k_sig, v_sig = jax.nn.sigmoid(q_conv), jax.nn.sigmoid(k_conv), jax.nn.sigmoid(v_conv)
    q_act, k_act, v_act = q_conv * q_sig, k_conv * k_sig, v_conv * v_sig
    dq_all, dk_all, dv_all = [], [], []
    chunks = piece // CHUNK
    for head in range(PAIR):
        narrow, wide = slice(head * DK, (head + 1) * DK), slice(head * DV, (head + 1) * DV)
        query_unit, query_scale = units(q_act[:, narrow])
        queries = query_unit * DK**-0.5
        keys, key_scale = units(k_act[:, narrow])
        values = v_act[:, wide]
        incoming = incoming_ref[0, head]
        grad_state = leaving_ref[0, head].astype(F32)
        grad_queries, grad_keys, grad_values = [None] * chunks, [None] * chunks, [None] * chunks
        for chunk in reversed(range(chunks)):
            part = slice(chunk * CHUNK, (chunk + 1) * CHUNK)
            query, key, value = queries[part], keys[part], values[part]
            beta, strict, causal, grow, fade, closing = fades(
                decay_ref[head, :, part], beta_ref[head, :, part], rows, cols
            )
            both = mm_nt(jnp.concatenate([key, query], axis=0), key)
            cross = both[:CHUNK] * strict
            lower = beta * cross
            scores = both[CHUNK:] * causal
            inverse = inverse_ref[part, head * CHUNK : (head + 1) * CHUNK]
            if chunk == 0:
                state = incoming.astype(F32)
            else:
                before = states_ref[0, head, chunk - 1]
                state = before[:, :DV].astype(F32) + mm(before[:, DV:], incoming)
            grad = grad_ref[part, wide]
            seen = mm(key, state)
            plain = value - grow * seen
            fresh = mm(inverse, beta * plain)
            tail = key * fade
            lifted = query * grow
            grad_fresh = mm_tn(scores, grad) + mm(tail, grad_state)
            grad_right = mm_tn(inverse, grad_fresh)
            grad_seen = -(beta * grow) * grad_right
            pair = mm_nt(jnp.concatenate([grad.astype(F32), grad_right], axis=0), fresh)
            grad_scores = jnp.where(rows >= cols, pair[:CHUNK], 0.0)
            grad_lower = jnp.where(rows > cols, -pair[CHUNK:], 0.0)
            pair = mm_nt(jnp.concatenate([grad.astype(F32), grad_seen], axis=0), state)
            grad_lifted, grad_key = pair[:CHUNK], pair[CHUNK:]
            grad_tail = mm_nt(fresh, grad_state)
            grad_cross = grad_lower * strict * beta
            grad_both = grad_scores * causal
            grad_query = mm(grad_both, key) + grad_lifted * grow
            grad_key = (
                grad_key
                + mm(grad_cross, key)
                + mm_tn(jnp.concatenate([grad_cross, grad_both], axis=0), jnp.concatenate([key, query], axis=0))
                + grad_tail * fade
            )
            spread = grad_lower * lower + grad_scores * scores
            tail_sum = jnp.sum(grad_tail * tail, axis=1, keepdims=True)
            grad_cumul = (
                jnp.sum(spread, axis=1, keepdims=True)
                - to_column(jnp.sum(spread, axis=0, keepdims=True), rows, cols)
                + jnp.sum(grad_lifted * lifted, axis=1, keepdims=True)
                - tail_sum
                + jnp.sum(grad_seen * seen, axis=1, keepdims=True)
            )
            grad_last = jnp.sum(tail_sum, axis=0, keepdims=True) + closing * jnp.sum(
                jnp.sum(state * grad_state, axis=1, keepdims=True), axis=0, keepdims=True
            )
            ddecay_ref[head, :, part] = (
                jnp.sum(jnp.where(rows >= cols, grad_cumul, 0.0), axis=0, keepdims=True) + grad_last
            )
            grad_beta = jnp.sum(grad_right * plain, axis=1, keepdims=True) + jnp.sum(
                grad_lower * cross, axis=1, keepdims=True
            )
            dbeta_ref[head, :, part] = to_row(grad_beta, rows, cols)
            grad_state = (
                closing * grad_state
                + mm_tn(jnp.concatenate([lifted, key], axis=0), jnp.concatenate([grad.astype(F32), grad_seen], axis=0))
            )
            grad_queries[chunk], grad_keys[chunk], grad_values[chunk] = grad_query, grad_key, beta * grad_right
        dq, dk, dv = (
            jnp.concatenate(grad_queries, axis=0) * DK**-0.5,
            jnp.concatenate(grad_keys, axis=0),
            jnp.concatenate(grad_values, axis=0),
        )
        dq_all.append(query_scale * (dq - query_unit * jnp.sum(dq * query_unit, axis=-1, keepdims=True)))
        dk_all.append(key_scale * (dk - keys * jnp.sum(dk * keys, axis=-1, keepdims=True)))
        dv_all.append(dv)
    dq = jnp.concatenate(dq_all, axis=1) * silu_slope(q_conv, q_sig)
    dk = jnp.concatenate(dk_all, axis=1) * silu_slope(k_conv, k_sig)
    dv = jnp.concatenate(dv_all, axis=1) * silu_slope(v_conv, v_sig)
    unconvolve(dq, qf_ref[...], held_q, back_q, piece, dq_ref, dqe_ref, dqf_ref)
    unconvolve(dk, kf_ref[...], held_k, back_k, piece, dk_ref, dke_ref, dkf_ref)
    unconvolve(dv, vf_ref[...], held_v, back_v, piece, dv_ref, dve_ref, dvf_ref)


def column_specs(rows, first_axis):
    steps = HEADS // PAIR
    return [
        pl.BlockSpec((rows, PAIR * DK), lambda h, s: (s if first_axis else 0, h)),
        pl.BlockSpec((rows, PAIR * DK), lambda h, s: (s if first_axis else 0, steps + h)),
        pl.BlockSpec((rows, PAIR * DV), lambda h, s: (s if first_axis else 0, steps + h)),
    ]


def gate_spec(piece):
    return pl.BlockSpec((PAIR, 1, piece), lambda h, s: (h, 0, s))


def rows_spec(piece, width):
    return pl.BlockSpec((piece, PAIR * width), lambda h, s: (s, h))


def head_spec(*shape):
    zeros = (0,) * len(shape)
    return pl.BlockSpec((1, PAIR) + shape, lambda h, s: (s, h) + zeros)


def params():
    return pltpu.CompilerParams(vmem_limit_bytes=VMEM, dimension_semantics=("arbitrary", "arbitrary"))


def shape_of(shape, dtype):
    return jax.ShapeDtypeStruct(shape, dtype)


def held(piece, extra):
    return [pltpu.VMEM((piece + extra, PAIR * width), F32) for width in (DK, DK, DV)]


def open_rule(projected, edges, taps, betas, decays, seqs, piece):
    rows, chunks = seqs * piece, piece // CHUNK
    return pl.pallas_call(
        functools.partial(opening_kernel, piece),
        grid=(HEADS // PAIR, seqs),
        in_specs=column_specs(piece, True) + column_specs(8, True) + column_specs(8, False)
        + [gate_spec(piece), gate_spec(piece)],
        out_specs=[rows_spec(piece, DV), rows_spec(piece, DK), head_spec(chunks, DK, WIDE), rows_spec(piece, CHUNK)],
        out_shape=[
            shape_of((rows, HEADS * DV), F32),
            shape_of((rows, HEADS * DK), BF),
            shape_of((seqs, HEADS, chunks, DK, WIDE), BF),
            shape_of((rows, HEADS * CHUNK), BF),
        ],
        scratch_shapes=held(piece, 8),
        compiler_params=params(),
        cost_estimate=pl.CostEstimate(flops=8 * 10**9, bytes_accessed=20 * 2**20, transcendentals=0),
        name="open_rule",
    )(projected, projected, projected, edges, edges, edges, taps, taps, taps, betas, decays)


def finish(local, reading, incoming, outgate, gain, seqs, piece):
    rows = seqs * piece
    return pl.pallas_call(
        finish_kernel,
        grid=(HEADS // PAIR, seqs),
        in_specs=[
            rows_spec(piece, DV), rows_spec(piece, DK), head_spec(DK, DV), rows_spec(piece, DV),
            pl.BlockSpec((8, DV), lambda h, s: (0, 0)),
        ],
        out_specs=[rows_spec(piece, DV), rows_spec(piece, DV)],
        out_shape=[shape_of((rows, HEADS * DV), F32), shape_of((rows, HEADS * DV), BF)],
        compiler_params=params(),
        name="finish_heads",
    )(local, reading, incoming, outgate, gain)


def unfinish(grad, mixed, outgate, gain, reading, seqs, piece):
    rows = seqs * piece
    return pl.pallas_call(
        unfinish_kernel,
        grid=(HEADS // PAIR, seqs),
        in_specs=[
            rows_spec(piece, DV), rows_spec(piece, DV), rows_spec(piece, DV),
            pl.BlockSpec((8, DV), lambda h, s: (0, 0)), rows_spec(piece, DK),
        ],
        out_specs=[rows_spec(piece, DV), rows_spec(piece, DV), head_spec(8, DV), head_spec(DK, DV)],
        out_shape=[
            shape_of((rows, HEADS * DV), BF), shape_of((rows, HEADS * DV), BF),
            shape_of((seqs, HEADS, 8, DV), F32), shape_of((seqs, HEADS, DK, DV), F32),
        ],
        compiler_params=params(),
        name="unfinish_heads",
    )(grad, mixed, outgate, gain, reading)


def close_rule(projected, edges, taps, betas, decays, inverse, states, incoming, grad, leaving, seqs, piece):
    rows, chunks = seqs * piece, piece // CHUNK
    sizes = (HEADS * DK, HEADS * DK, HEADS * DV)
    steps = HEADS // PAIR

    def blocks(height):
        return [pl.BlockSpec((height, PAIR * w), lambda h, s: (s, h)) for w in (DK, DK, DV)]

    return pl.pallas_call(
        functools.partial(closing_kernel, piece),
        grid=(steps, seqs),
        in_specs=column_specs(piece, True) + column_specs(8, True) + column_specs(8, False)
        + [gate_spec(piece), gate_spec(piece), rows_spec(piece, CHUNK), head_spec(chunks, DK, WIDE),
           head_spec(DK, DV), rows_spec(piece, DV), head_spec(DK, DV)],
        out_specs=blocks(piece) + blocks(8)
        + [pl.BlockSpec((1, 8, PAIR * w), lambda h, s: (s, 0, h)) for w in (DK, DK, DV)]
        + [gate_spec(piece), gate_spec(piece)],
        out_shape=[shape_of((rows, w), BF) for w in sizes]
        + [shape_of((seqs * 8, w), F32) for w in sizes]
        + [shape_of((seqs, 8, w), F32) for w in sizes]
        + [shape_of((HEADS, 1, rows), F32)] * 2,
        scratch_shapes=held(piece, 8) + held(piece, 16),
        compiler_params=params(),
        cost_estimate=pl.CostEstimate(flops=16 * 10**9, bytes_accessed=30 * 2**20, transcendentals=0),
        name="close_rule",
    )(projected, projected, projected, edges, edges, edges, taps, taps, taps, betas, decays,
      inverse, states, incoming, grad, leaving)


SEQ = ("y", "x")
ALL = ("z", "c", "y", "x")


def product(left, right):
    return jnp.dot(left, right, preferred_element_type=F32)


def product_left(left, right):
    return lax.dot_general(left, right, (((0,), (0,)), ((), ())), preferred_element_type=F32)


def product_right(left, right):
    return lax.dot_general(left, right, (((1,), (1,)), ((), ())), preferred_element_type=F32)


def inverse_root(value):
    return lax.rsqrt(jnp.mean(value * value, axis=-1, keepdims=True) + EPS)


def norm_back(grad, normed, inverse, gain):
    scaled = grad * gain
    return (
        jnp.sum(grad * normed, axis=0),
        inverse * (scaled - normed * jnp.mean(scaled * normed, axis=-1, keepdims=True)),
    )


def shift(block, distance):
    devices = range(lax.axis_size(SEQ))
    return lax.ppermute(block, SEQ, [(i - distance, i) for i in devices if i - distance in devices])


def take(block, dim, index):
    return lax.dynamic_index_in_dim(block, index, dim, keepdims=False)


def line_sum(parts, axis, dim):
    size, me = lax.axis_size(axis), lax.axis_index(axis)

    def share(index):
        index = jnp.clip(index, 0, size - 1)
        total = take(parts[0], dim, index).astype(F32)
        for part in parts[1:]:
            total = total + take(part, dim, index).astype(F32)
        return total

    from_left = from_right = None
    for step in range(1, size):
        right_going = share(me + size - step)
        left_going = share(me - size + step)
        if from_left is not None:
            right_going = right_going + from_left.astype(F32)
            left_going = left_going + from_right.astype(F32)
        from_left = lax.ppermute(right_going.astype(BF), axis, [(i, i + 1) for i in range(step) if i + 1 < size])
        from_right = lax.ppermute(
            left_going.astype(BF), axis, [(i, i - 1) for i in range(size - step, size) if i > 0]
        )
    return [share(me), from_left, from_right]


def scatter_sum(grad, order):
    sizes = [lax.axis_size(axis) for axis in ALL]
    rows = grad.shape[0] // (sizes[0] * sizes[1] * sizes[2] * sizes[3])
    parts = [grad.reshape(*sizes, rows, grad.shape[1])]
    left = list(ALL)
    for axis in order:
        dim = left.index(axis)
        me, size = lax.axis_index(axis), lax.axis_size(axis)
        if size == 2:
            total_other = sum_of([take(part, dim, 1 - me) for part in parts])
            total_mine = sum_of([take(part, dim, me) for part in parts])
            parts = [total_mine.astype(BF), lax.ppermute(total_other.astype(BF), axis, [(0, 1), (1, 0)])]
        else:
            parts = [part for part in line_sum(parts, axis, dim)]
        left.remove(axis)
    return sum_of(parts)


def sum_of(parts):
    total = parts[0].astype(F32)
    for part in parts[1:]:
        total = total + part.astype(F32)
    return total


def shards(
    tokens, cotangent, gain_mixer, proj_input, conv_filter, proj_gates, proj_outgate, gain_heads,
    proj_output, gain_feed, feed_gate, feed_up, feed_down, decay_log, decay_bias,
):
    seqs, piece = tokens.shape[0], tokens.shape[1]
    rows = seqs * piece
    width = HEADS * DK
    channels = 2 * width + HEADS * DV
    devices = lax.axis_size(ALL)
    own = proj_input.shape[0]

    extras = jnp.concatenate(
        [
            proj_gates,
            conv_filter.reshape(own, -1),
            gain_mixer[:, None],
            gain_feed[:, None],
            jnp.pad(gain_heads, (0, own - gain_heads.shape[0]))[:, None],
        ],
        axis=1,
    )
    extras = jnp.pad(extras, ((0, 0), (0, 128 - extras.shape[1])))
    group = lax.all_gather(jnp.concatenate([proj_input, proj_outgate, extras], axis=1), ALL, axis=0, tiled=True)
    output_matrix = lax.all_gather(proj_output, ALL, axis=0, tiled=True)
    feed_group = lax.all_gather(jnp.concatenate([feed_gate, feed_up], axis=1), ALL, axis=0, tiled=True)
    down_matrix = lax.all_gather(feed_down, ALL, axis=0, tiled=True)
    hidden_units = feed_gate.shape[1]

    input_matrix = group[:, :channels]
    outgate_matrix = group[:, channels : channels + HEADS * DV]
    small = group[:, channels + HEADS * DV :]
    gates_matrix = small[:, : 2 * HEADS]
    bank = small[:, 2 * HEADS : 2 * HEADS + 16].reshape(channels, CONV).astype(F32)
    gain_first = small[:, 2 * HEADS + 16].astype(F32)
    gain_second = small[:, 2 * HEADS + 17].astype(F32)
    heads_gain = small[:, 2 * HEADS + 18].reshape(devices, own)[:, : gain_heads.shape[0]].reshape(1, DV)
    heads_gain = jnp.broadcast_to(heads_gain.astype(F32), (8, DV))
    taps = jnp.pad(bank.T, ((0, 8 - CONV), (0, 0)))

    residual = tokens.astype(F32).reshape(rows, D)
    inverse_one = inverse_root(residual)
    normed_one = residual * inverse_one
    first = (normed_one * gain_first).astype(BF)
    projected = product(first, input_matrix).astype(BF)
    gate_pre = lax.dot_general(gates_matrix, first, (((0,), (1,)), ((), ())), preferred_element_type=F32)
    betas = jax.nn.sigmoid(gate_pre[:HEADS])
    decay_pre = gate_pre[HEADS:] + decay_bias[:, None]
    rates = jnp.exp(decay_log)[:, None]
    decays = -rates * jax.nn.softplus(decay_pre)
    beta_rows, decay_rows = betas.reshape(HEADS, 1, rows), decays.reshape(HEADS, 1, rows)
    edge = shift(projected.reshape(seqs, piece, channels)[:, piece - CONV + 1 :], 1)
    edges = jnp.pad(edge.astype(F32), ((0, 0), (9 - CONV, 0), (0, 0))).reshape(seqs * 8, channels)
    local, reading, states, inverse = open_rule(projected, edges, taps, beta_rows, decay_rows, seqs, piece)
    outgate = product(first, outgate_matrix)

    pieces = lax.axis_size(SEQ)
    carried, transfer = states[:, :, -1, :, :DV], states[:, :, -1, :, DV:]
    incoming = jnp.zeros(carried.shape, BF)
    for hop in range(1, pieces):
        ending = carried.astype(F32) + jnp.einsum(
            "...dk,...ke->...de", transfer, incoming, preferred_element_type=F32
        )
        incoming = incoming + lax.ppermute(ending.astype(BF), SEQ, [(hop - 1, hop)])

    mixed, gated = finish(local, reading, incoming, outgate, heads_gain, seqs, piece)
    middle = residual + product(gated, output_matrix)
    inverse_two = inverse_root(middle)
    normed_two = middle * inverse_two
    second = (normed_two * gain_second).astype(BF)
    gate_matrix, upward_matrix = feed_group[:, :hidden_units], feed_group[:, hidden_units:]
    up_gate = product(second, gate_matrix)
    up_linear = product(second, upward_matrix)
    sigmoid_gate = jax.nn.sigmoid(up_gate)
    silu_gate = up_gate * sigmoid_gate
    hidden = (silu_gate * up_linear).astype(BF)
    layer_out = (middle + product(hidden, down_matrix)).astype(BF)

    grad_branch = cotangent.reshape(rows, D)
    grad_feed_down = product_left(hidden, grad_branch).astype(BF)
    grad_hidden = product_right(grad_branch, down_matrix)
    grad_gate = (grad_hidden * up_linear * (sigmoid_gate + silu_gate * (1.0 - sigmoid_gate))).astype(BF)
    grad_up = (grad_hidden * silu_gate).astype(BF)
    grad_feed_gate = product_left(second, grad_gate).astype(BF)
    grad_feed_up = product_left(second, grad_up).astype(BF)
    sum_feed_down = scatter_sum(grad_feed_down, ("c", "z", "x", "y"))
    sum_feed_gate = scatter_sum(grad_feed_gate, ("c", "x", "y", "z"))
    sum_feed_up = scatter_sum(grad_feed_up, ("c", "y", "x", "z"))
    grad_second = product_right(grad_gate, gate_matrix) + product_right(grad_up, upward_matrix)
    grad_gain_feed, grad_norm_two = norm_back(grad_second, normed_two, inverse_two, gain_second)
    grad_middle = grad_branch.astype(F32) + grad_norm_two
    grad_mixer_out = grad_middle.astype(BF)
    grad_proj_output = product_left(gated, grad_mixer_out).astype(BF)
    sum_proj_output = scatter_sum(grad_proj_output, ("c", "x", "y", "z"))
    grad_gated = product_right(grad_mixer_out, output_matrix)
    grad_mixed, grad_outgate, gain_parts, flow = unfinish(
        grad_gated, mixed, outgate, heads_gain, reading, seqs, piece
    )
    grad_gain_heads = jnp.sum(gain_parts[:, :, 0], axis=(0, 1))
    grad_proj_outgate = product_left(first, grad_outgate).astype(BF)
    sum_proj_outgate = scatter_sum(grad_proj_outgate, ("c", "y", "x", "z"))

    leaving = jnp.zeros(carried.shape, BF)
    for hop in range(pieces - 1, 0, -1):
        starting = flow + jnp.einsum("...ki,...ke->...ie", transfer, leaving, preferred_element_type=F32)
        leaving = leaving + lax.ppermute(starting.astype(BF), SEQ, [(hop, hop - 1)])

    outs = close_rule(
        projected, edges, taps, beta_rows, decay_rows, inverse, states, incoming, grad_mixed, leaving, seqs, piece
    )
    grad_edges = jnp.concatenate(outs[3:6], axis=1).reshape(seqs, 8, channels)[:, 9 - CONV :]
    returned = shift(grad_edges.astype(BF), -1)
    starts = (0, width, 2 * width, channels)
    grad_parts = []
    for part, grad in enumerate(outs[:3]):
        back = returned[:, :, starts[part] : starts[part + 1]]
        grad = grad.reshape(seqs, piece, -1)
        tail = (grad[:, piece - 8 :].astype(F32) + jnp.pad(back.astype(F32), ((0, 0), (9 - CONV, 0), (0, 0)))).astype(BF)
        grad_parts.append(lax.dynamic_update_slice(grad, tail, (0, piece - 8, 0)).reshape(rows, -1))
    bank_grad = jnp.concatenate(outs[6:9], axis=2).sum(axis=0)[:CONV].T
    grad_betas, grad_decays = outs[9].reshape(HEADS, rows), outs[10].reshape(HEADS, rows)
    grad_beta_pre = grad_betas * betas * (1.0 - betas)
    grad_decay_pre = -rates * grad_decays * jax.nn.sigmoid(decay_pre)
    grad_decay_log = jnp.sum(grad_decays * decays, axis=1)
    grad_decay_bias = jnp.sum(grad_decay_pre, axis=1)
    grad_gates = jnp.concatenate([grad_beta_pre, grad_decay_pre], axis=0).astype(BF)

    orders = (("c", "z", "x", "y"), ("c", "x", "y", "z"), ("c", "y", "x", "z"))
    sums = [
        scatter_sum(product_left(first, grad).astype(BF), order) for grad, order in zip(grad_parts, orders)
    ]
    sum_proj_input = jnp.concatenate(sums, axis=1)
    grad_first = (
        product_right(grad_outgate, outgate_matrix)
        + lax.dot_general(grad_gates, gates_matrix, (((0,), (1,)), ((), ())), preferred_element_type=F32)
    )
    for part, grad in enumerate(grad_parts):
        grad_first = grad_first + product_right(grad, input_matrix[:, starts[part] : starts[part + 1]])
    grad_gain_mixer, grad_norm_one = norm_back(grad_first, normed_one, inverse_one, gain_first)
    tokens_grad = (grad_middle + grad_norm_one).reshape(seqs, piece, D)
    grad_proj_gates = lax.dot_general(first, grad_gates, (((0,), (1,)), ((), ())), preferred_element_type=F32)

    pieces_small = (
        grad_gain_mixer, grad_gain_feed, grad_gain_heads, grad_decay_log, grad_decay_bias,
        bank_grad.reshape(-1), grad_proj_gates.reshape(-1),
    )
    packed = jnp.concatenate(pieces_small)
    packed = lax.psum(jnp.pad(packed, (0, -packed.shape[0] % 1024)), ALL)
    me = lax.axis_index(ALL)
    found, place = [], 0
    for block in pieces_small:
        size = block.shape[0]
        if size == HEADS:
            found.append(packed[place : place + size])
        else:
            found.append(lax.dynamic_slice(packed, (place + me * (size // devices),), (size // devices,)))
        place += size
    return (
        layer_out.reshape(seqs, piece, D),
        tokens_grad,
        found[0],
        sum_proj_input,
        found[5].reshape(-1, CONV),
        found[6].reshape(-1, 2 * HEADS),
        sum_proj_outgate,
        found[2],
        sum_proj_output,
        found[1],
        sum_feed_gate,
        sum_feed_up,
        sum_feed_down,
        found[3],
        found[4],
    )


def solution(mesh):
    dp, seq = mesh.shape["dp"], mesh.shape["seq"]
    side = math.isqrt(seq)
    side = side if side * side == seq else 1
    fine = jax.sharding.Mesh(mesh.devices.reshape(dp // 2, 2, seq // side, side), ALL)
    row, vector, split = P(("z", "c"), SEQ, None), P(ALL), P(ALL, None)
    in_specs = (row, row, vector, split, split, split, split, vector, split, vector, split, split, split, P(), P())
    out_specs = (row, row, vector, split, split, split, split, vector, split, vector, split, split, split, P(), P())
    return jax.shard_map(shards, mesh=fine, in_specs=in_specs, out_specs=out_specs, check_vma=False)
```

```python
import functools
import math
import jax
import jax.numpy as jnp
from jax import lax
from jax.experimental import pallas as pl
from jax.experimental.pallas import tpu as pltpu
from jax.sharding import PartitionSpec as P

D = 1024
HEADS = 8
DK = 128
DV = 256
CONV = 4
CHUNK = 128
PAIR = 2
EPS = 1e-06
WIDE = DV + DK
VMEM = 56 * 1024 * 1024
BF = jnp.bfloat16
F32 = jnp.float32


def dot(left, right, over):
    return lax.dot_general(left, right, (((over[0],), (over[1],)), ((), ())), preferred_element_type=F32)


def split(value):
    if value.dtype == BF:
        return value, None
    high = value.astype(BF)
    return high, (value - high.astype(F32)).astype(BF)


def mm(left, right, over=(1, 0)):
    (left, left_low), (right, right_low) = split(left), split(right)
    total = dot(left, right, over)
    if left_low is not None:
        total = total + dot(left_low, right, over)
    if right_low is not None:
        total = total + dot(left, right_low, over)
    return total


def mm_nt(left, right):
    return mm(left, right, (1, 1))


def mm_tn(left, right):
    return mm(left, right, (0, 0))


def grids():
    rows = lax.broadcasted_iota(jnp.int32, (CHUNK, CHUNK), 0)
    cols = lax.broadcasted_iota(jnp.int32, (CHUNK, CHUNK), 1)
    return rows, cols


def to_column(row, rows, cols):
    return jnp.sum(jnp.where(rows == cols, row, 0.0), axis=1, keepdims=True)


def to_row(column, rows, cols):
    return jnp.sum(jnp.where(rows == cols, column, 0.0), axis=0, keepdims=True)


def fades(decay_row, beta_row, rows, cols):
    cumul = jnp.sum(jnp.where(cols <= rows, decay_row, 0.0), axis=1, keepdims=True)
    cumul_row = to_row(cumul, rows, cols)
    beta = to_column(beta_row, rows, cols)
    fading = jnp.exp(jnp.minimum(cumul - cumul_row, 0.0))
    strict = jnp.where(rows > cols, fading, 0.0)
    causal = jnp.where(rows >= cols, fading, 0.0)
    last = cumul[CHUNK - 1 : CHUNK]
    return beta, strict, causal, jnp.exp(cumul), jnp.exp(last - cumul), jnp.exp(last)


def unit_lower_inverses(lowers, rows, cols):
    def level(lower, width):
        shift = width.bit_length() - 1
        row_block, col_block = lax.shift_right_logical(rows, shift), lax.shift_right_logical(cols, shift)
        return jnp.where((row_block == col_block + 1) & ((col_block & 1) == 0), lower, 0.0)

    inverses = [jnp.where(rows == cols, 1.0, 0.0) - level(lower, 1) for lower in lowers]
    width = 2
    while width < CHUNK:
        steps = [mm(inverse, level(lower, width)) for inverse, lower in zip(inverses, lowers)]
        steps = [mm(step, inverse) for inverse, step in zip(inverses, steps)]
        inverses = [inverse - step for inverse, step in zip(inverses, steps)]
        width *= 2
    return inverses


def convolve(x, edge, taps, held, piece):
    held[0:8] = edge
    held[8 : 8 + piece] = x.astype(F32)
    total = taps[0:1] * held[5 : 5 + piece]
    for j in range(1, CONV):
        total = total + taps[j : j + 1] * held[5 + j : 5 + j + piece]
    return total


def units(active):
    inverse = lax.rsqrt(jnp.sum(active * active, axis=-1, keepdims=True) + EPS)
    return active * inverse, inverse


def opening_kernel(
    piece, q_ref, k_ref, v_ref, qe_ref, ke_ref, ve_ref, qf_ref, kf_ref, vf_ref, beta_ref, decay_ref,
    local_ref, reading_ref, states_ref, inverse_ref, held_q, held_k, held_v,
):
    rows, cols = grids()
    q_conv = convolve(q_ref[...], qe_ref[...], qf_ref[...], held_q, piece)
    k_conv = convolve(k_ref[...], ke_ref[...], kf_ref[...], held_k, piece)
    v_conv = convolve(v_ref[...], ve_ref[...], vf_ref[...], held_v, piece)
    q_act = q_conv * jax.nn.sigmoid(q_conv)
    k_act = k_conv * jax.nn.sigmoid(k_conv)
    v_act = v_conv * jax.nn.sigmoid(v_conv)
    chunks = piece // CHUNK
    parts = [slice(chunk * CHUNK, (chunk + 1) * CHUNK) for chunk in range(chunks)]
    terms = {}
    for head in range(PAIR):
        queries = units(q_act[:, head * DK : (head + 1) * DK])[0] * DK**-0.5
        keys = units(k_act[:, head * DK : (head + 1) * DK])[0]
        for chunk, part in enumerate(parts):
            query, key = queries[part], keys[part]
            beta, strict, causal, grow, fade, closing = fades(
                decay_ref[head, :, part], beta_ref[head, :, part], rows, cols
            )
            both = mm_nt(jnp.concatenate([key, query], axis=0), key)
            value = beta * v_act[part, head * DV : (head + 1) * DV]
            terms[head, chunk] = (
                beta * both[:CHUNK] * strict,
                both[CHUNK:] * causal,
                jnp.concatenate([key * (beta * grow), query * grow], axis=0),
                key * fade,
                jnp.concatenate([value, jnp.zeros((CHUNK, DK), F32)], axis=1),
                closing,
            )
    inverses = unit_lower_inverses([term[0] for term in terms.values()], rows, cols)
    inverses = dict(zip(terms, inverses))
    opening = jnp.concatenate([jnp.zeros((DK, DV), F32), jnp.where(rows == cols, 1.0, 0.0)], axis=1)
    held_states = [opening] * PAIR
    for chunk, part in enumerate(parts):
        for head in range(PAIR):
            _, scores, looking, tail, value, closing = terms[head, chunk]
            inverse, state = inverses[head, chunk], held_states[head]
            inverse_ref[part, head * CHUNK : (head + 1) * CHUNK] = inverse
            seen = mm(looking, state)
            fresh = mm(inverse, value - seen[:CHUNK])
            result = seen[CHUNK:] + mm(scores, fresh)
            state = closing * state + mm_tn(tail, fresh)
            held_states[head] = state
            local_ref[part, head * DV : (head + 1) * DV] = result[:, :DV]
            reading_ref[part, head * DK : (head + 1) * DK] = result[:, DV:]
            states_ref[0, head, chunk] = state


def finish_kernel(local_ref, reading_ref, incoming_ref, outgate_ref, gain_ref, mixed_ref, gated_ref):
    for head in range(PAIR):
        wide = slice(head * DV, (head + 1) * DV)
        mixed = local_ref[:, wide] + mm(reading_ref[:, head * DK : (head + 1) * DK], incoming_ref[0, head])
        mixed_ref[:, wide] = mixed
        inverse = lax.rsqrt(jnp.mean(mixed * mixed, axis=-1, keepdims=True) + EPS)
        outgate = outgate_ref[:, wide]
        gated = mixed * inverse * gain_ref[0:1] * (outgate * jax.nn.sigmoid(outgate))
        gated_ref[:, wide] = gated.astype(BF)


def unfinish_kernel(
    grad_ref, mixed_ref, outgate_ref, gain_ref, reading_ref, grad_mixed_ref, grad_outgate_ref, gain_grad_ref, flow_ref
):
    gain = gain_ref[0:1]
    for head in range(PAIR):
        wide = slice(head * DV, (head + 1) * DV)
        mixed, outgate, grad = mixed_ref[:, wide], outgate_ref[:, wide], grad_ref[:, wide]
        inverse = lax.rsqrt(jnp.mean(mixed * mixed, axis=-1, keepdims=True) + EPS)
        normed = mixed * inverse
        sigmoid = jax.nn.sigmoid(outgate)
        gate = outgate * sigmoid
        along = grad * normed
        gain_grad = jnp.sum(along * gate, axis=0, keepdims=True)
        gain_grad_ref[0, head] = jnp.broadcast_to(gain_grad, (8, DV))
        grad_outgate_ref[:, wide] = (along * gain * (sigmoid + gate * (1.0 - sigmoid))).astype(BF)
        scaled = grad * gain * gate
        grad_mixed = inverse * (scaled - normed * jnp.mean(scaled * normed, axis=-1, keepdims=True))
        grad_mixed_ref[:, wide] = grad_mixed
        flow_ref[0, head] = mm_tn(reading_ref[:, head * DK : (head + 1) * DK], grad_mixed)


def unconvolve(grad, taps, held_in, held_out, piece, grad_ref, edge_ref, taps_ref):
    width = grad.shape[1]
    held_out[0:8] = jnp.zeros((8, width), F32)
    held_out[8 : 8 + piece] = grad
    held_out[8 + piece : 16 + piece] = jnp.zeros((8, width), F32)
    total = taps[0:1] * held_out[11 : 11 + piece]
    edge = taps[0:1] * held_out[3:11]
    for j in range(1, CONV):
        total = total + taps[j : j + 1] * held_out[11 - j : 11 - j + piece]
        edge = edge + taps[j : j + 1] * held_out[3 - j : 11 - j]
    grad_ref[...] = total.astype(BF)
    edge_ref[...] = edge
    sums = [jnp.sum(grad * held_in[5 + j : 5 + j + piece], axis=0, keepdims=True) for j in range(CONV)]
    taps_ref[0] = jnp.concatenate(sums + [jnp.zeros((8 - CONV, width), F32)], axis=0)


def silu_slope(value, sigmoid):
    return sigmoid * (1.0 + value * (1.0 - sigmoid))


def closing_kernel(
    piece, q_ref, k_ref, v_ref, qe_ref, ke_ref, ve_ref, qf_ref, kf_ref, vf_ref, beta_ref, decay_ref,
    inverse_ref, states_ref, incoming_ref, grad_ref, leaving_ref,
    dq_ref, dk_ref, dv_ref, dqe_ref, dke_ref, dve_ref, dqf_ref, dkf_ref, dvf_ref, dbeta_ref, ddecay_ref,
    held_q, held_k, held_v, back_q, back_k, back_v,
):
    rows, cols = grids()
    q_conv = convolve(q_ref[...], qe_ref[...], qf_ref[...], held_q, piece)
    k_conv = convolve(k_ref[...], ke_ref[...], kf_ref[...], held_k, piece)
    v_conv = convolve(v_ref[...], ve_ref[...], vf_ref[...], held_v, piece)
    q_sig, k_sig, v_sig = jax.nn.sigmoid(q_conv), jax.nn.sigmoid(k_conv), jax.nn.sigmoid(v_conv)
    q_act, k_act, v_act = q_conv * q_sig, k_conv * k_sig, v_conv * v_sig
    chunks = piece // CHUNK
    parts = [slice(chunk * CHUNK, (chunk + 1) * CHUNK) for chunk in range(chunks)]
    narrows = [slice(head * DK, (head + 1) * DK) for head in range(PAIR)]
    wides = [slice(head * DV, (head + 1) * DV) for head in range(PAIR)]
    places = [(head, chunk) for chunk in reversed(range(chunks)) for head in range(PAIR)]
    unit_parts = [units(q_act[:, narrow]) + units(k_act[:, narrow]) for narrow in narrows]
    terms = {}
    for head, chunk in places:
        part = parts[chunk]
        query, key = unit_parts[head][0][part] * DK**-0.5, unit_parts[head][2][part]
        beta, strict, causal, grow, fade, closing = fades(
            decay_ref[head, :, part], beta_ref[head, :, part], rows, cols
        )
        both = mm_nt(jnp.concatenate([key, query], axis=0), key)
        scores = both[CHUNK:] * causal
        incoming = incoming_ref[0, head]
        if chunk == 0:
            state = incoming.astype(F32)
        else:
            before = states_ref[0, head, chunk - 1]
            state = before[:, :DV] + mm(before[:, DV:], incoming)
        seen = mm(key, state)
        grad = grad_ref[part, wides[head]]
        terms[head, chunk] = dict(
            query=query, key=key, beta=beta, strict=strict, causal=causal, grow=grow, fade=fade, closing=closing,
            cross=both[:CHUNK] * strict, scores=scores, state=state, seen=seen, grad=grad,
            plain=v_act[part, wides[head]] - grow * seen,
            inverse=inverse_ref[part, head * CHUNK : (head + 1) * CHUNK],
            grad_fresh=mm_tn(scores, grad), grad_state=mm_tn(query * grow, grad),
        )
    for place in places:
        term = terms[place]
        term["fresh"] = mm(term["inverse"], term["beta"] * term["plain"])
    grad_states = [leaving_ref[0, head].astype(F32) for head in range(PAIR)]
    for place in places:
        term, grad_state = terms[place], grad_states[place[0]]
        key = term["key"]
        grad_fresh = term["grad_fresh"] + mm(key * term["fade"], grad_state)
        grad_right = mm_tn(term["inverse"], grad_fresh)
        term["grad_right"], term["grad_seen"] = grad_right, -(term["beta"] * term["grow"]) * grad_right
        term["grad_after"] = grad_state
        grad_states[place[0]] = term["closing"] * grad_state + term["grad_state"] + mm_tn(key, term["grad_seen"])
    for head, chunk in places:
        term, part = terms[head, chunk], parts[chunk]
        query, key, beta, strict, causal, grow, fade, closing, cross, scores, state, seen, grad = [
            term[name]
            for name in (
                "query", "key", "beta", "strict", "causal", "grow", "fade", "closing", "cross", "scores", "state",
                "seen", "grad",
            )
        ]
        grad_right, grad_seen, grad_state, fresh = [
            term[name] for name in ("grad_right", "grad_seen", "grad_after", "fresh")
        ]
        pair = mm_nt(jnp.concatenate([grad, grad_right], axis=0), fresh)
        grad_scores = jnp.where(rows >= cols, pair[:CHUNK], 0.0)
        grad_lower = jnp.where(rows > cols, -pair[CHUNK:], 0.0)
        pair = mm_nt(jnp.concatenate([grad, grad_seen], axis=0), state)
        grad_lifted, grad_key = pair[:CHUNK], pair[CHUNK:]
        grad_tail = mm_nt(fresh, grad_state)
        grad_cross = grad_lower * strict * beta
        grad_both = grad_scores * causal
        term["grad_query"] = mm(grad_both, key) + grad_lifted * grow
        term["grad_key"] = (
            grad_key
            + mm(grad_cross, key)
            + mm_tn(jnp.concatenate([grad_cross, grad_both], axis=0), jnp.concatenate([key, query], axis=0))
            + grad_tail * fade
        )
        spread = grad_lower * beta * cross + grad_scores * scores
        tail_sum = jnp.sum(grad_tail * (key * fade), axis=1, keepdims=True)
        grad_cumul = (
            jnp.sum(spread, axis=1, keepdims=True)
            - to_column(jnp.sum(spread, axis=0, keepdims=True), rows, cols)
            + jnp.sum(grad_lifted * (query * grow) - grad_tail * (key * fade), axis=1, keepdims=True)
            + jnp.sum(grad_seen * seen, axis=1, keepdims=True)
        )
        grad_last = jnp.sum(tail_sum, axis=0, keepdims=True) + closing * jnp.sum(
            jnp.sum(state * grad_state, axis=0, keepdims=True), axis=1, keepdims=True
        )
        ddecay_ref[head, :, part] = (
            jnp.sum(jnp.where(rows >= cols, grad_cumul, 0.0), axis=0, keepdims=True) + grad_last
        )
        grad_beta = jnp.sum(grad_right * term["plain"], axis=1, keepdims=True) + jnp.sum(
            grad_lower * cross, axis=1, keepdims=True
        )
        dbeta_ref[head, :, part] = to_row(grad_beta, rows, cols)
    dq_all, dk_all, dv_all = [], [], []
    for head in range(PAIR):
        query_unit, query_scale, keys, key_scale = unit_parts[head]
        dq, dk = [
            jnp.concatenate([terms[head, chunk][name] for chunk in range(chunks)], axis=0)
            for name in ("grad_query", "grad_key")
        ]
        dq = dq * DK**-0.5
        dq_all.append(query_scale * (dq - query_unit * jnp.sum(dq * query_unit, axis=-1, keepdims=True)))
        dk_all.append(key_scale * (dk - keys * jnp.sum(dk * keys, axis=-1, keepdims=True)))
        dv_all.append(
            jnp.concatenate(
                [terms[head, chunk]["beta"] * terms[head, chunk]["grad_right"] for chunk in range(chunks)], axis=0
            )
        )
    dq = jnp.concatenate(dq_all, axis=1) * silu_slope(q_conv, q_sig)
    dk = jnp.concatenate(dk_all, axis=1) * silu_slope(k_conv, k_sig)
    dv = jnp.concatenate(dv_all, axis=1) * silu_slope(v_conv, v_sig)
    unconvolve(dq, qf_ref[...], held_q, back_q, piece, dq_ref, dqe_ref, dqf_ref)
    unconvolve(dk, kf_ref[...], held_k, back_k, piece, dk_ref, dke_ref, dkf_ref)
    unconvolve(dv, vf_ref[...], held_v, back_v, piece, dv_ref, dve_ref, dvf_ref)


def column_specs(rows, first_axis):
    steps = HEADS // PAIR
    return [
        pl.BlockSpec((rows, PAIR * DK), lambda h, s: (s if first_axis else 0, h)),
        pl.BlockSpec((rows, PAIR * DK), lambda h, s: (s if first_axis else 0, steps + h)),
        pl.BlockSpec((rows, PAIR * DV), lambda h, s: (s if first_axis else 0, steps + h)),
    ]


def gate_spec(piece):
    return pl.BlockSpec((PAIR, 1, piece), lambda h, s: (h, 0, s))


def rows_spec(piece, width):
    return pl.BlockSpec((piece, PAIR * width), lambda h, s: (s, h))


def head_spec(*shape):
    zeros = (0,) * len(shape)
    return pl.BlockSpec((1, PAIR) + shape, lambda h, s: (s, h) + zeros)


def params():
    return pltpu.CompilerParams(vmem_limit_bytes=VMEM, dimension_semantics=("arbitrary", "arbitrary"))


def shape_of(shape, dtype):
    return jax.ShapeDtypeStruct(shape, dtype)


def held(piece, extra):
    return [pltpu.VMEM((piece + extra, PAIR * width), F32) for width in (DK, DK, DV)]


def open_rule(projected, edges, taps, betas, decays, seqs, piece):
    rows, chunks = seqs * piece, piece // CHUNK
    return pl.pallas_call(
        functools.partial(opening_kernel, piece),
        grid=(HEADS // PAIR, seqs),
        in_specs=column_specs(piece, True) + column_specs(8, True) + column_specs(8, False)
        + [gate_spec(piece), gate_spec(piece)],
        out_specs=[rows_spec(piece, DV), rows_spec(piece, DK), head_spec(chunks, DK, WIDE), rows_spec(piece, CHUNK)],
        out_shape=[
            shape_of((rows, HEADS * DV), F32),
            shape_of((rows, HEADS * DK), F32),
            shape_of((seqs, HEADS, chunks, DK, WIDE), F32),
            shape_of((rows, HEADS * CHUNK), F32),
        ],
        scratch_shapes=held(piece, 8),
        compiler_params=params(),
        cost_estimate=pl.CostEstimate(flops=30 * 10**9, bytes_accessed=20 * 2**20, transcendentals=0),
        name="open_rule",
    )(projected, projected, projected, edges, edges, edges, taps, taps, taps, betas, decays)


def finish(local, reading, incoming, outgate, gain, seqs, piece):
    rows = seqs * piece
    return pl.pallas_call(
        finish_kernel,
        grid=(HEADS // PAIR, seqs),
        in_specs=[
            rows_spec(piece, DV), rows_spec(piece, DK), head_spec(DK, DV), rows_spec(piece, DV),
            pl.BlockSpec((8, DV), lambda h, s: (0, 0)),
        ],
        out_specs=[rows_spec(piece, DV), rows_spec(piece, DV)],
        out_shape=[shape_of((rows, HEADS * DV), F32), shape_of((rows, HEADS * DV), BF)],
        compiler_params=params(),
        name="finish_heads",
    )(local, reading, incoming, outgate, gain)


def unfinish(grad, mixed, outgate, gain, reading, seqs, piece):
    rows = seqs * piece
    return pl.pallas_call(
        unfinish_kernel,
        grid=(HEADS // PAIR, seqs),
        in_specs=[
            rows_spec(piece, DV), rows_spec(piece, DV), rows_spec(piece, DV),
            pl.BlockSpec((8, DV), lambda h, s: (0, 0)), rows_spec(piece, DK),
        ],
        out_specs=[rows_spec(piece, DV), rows_spec(piece, DV), head_spec(8, DV), head_spec(DK, DV)],
        out_shape=[
            shape_of((rows, HEADS * DV), F32), shape_of((rows, HEADS * DV), BF),
            shape_of((seqs, HEADS, 8, DV), F32), shape_of((seqs, HEADS, DK, DV), F32),
        ],
        compiler_params=params(),
        name="unfinish_heads",
    )(grad, mixed, outgate, gain, reading)


def close_rule(projected, edges, taps, betas, decays, inverse, states, incoming, grad, leaving, seqs, piece):
    rows, chunks = seqs * piece, piece // CHUNK
    sizes = (HEADS * DK, HEADS * DK, HEADS * DV)
    steps = HEADS // PAIR

    def blocks(height):
        return [pl.BlockSpec((height, PAIR * w), lambda h, s: (s, h)) for w in (DK, DK, DV)]

    return pl.pallas_call(
        functools.partial(closing_kernel, piece),
        grid=(steps, seqs),
        in_specs=column_specs(piece, True) + column_specs(8, True) + column_specs(8, False)
        + [gate_spec(piece), gate_spec(piece), rows_spec(piece, CHUNK), head_spec(chunks, DK, WIDE),
           head_spec(DK, DV), rows_spec(piece, DV), head_spec(DK, DV)],
        out_specs=blocks(piece) + blocks(8)
        + [pl.BlockSpec((1, 8, PAIR * w), lambda h, s: (s, 0, h)) for w in (DK, DK, DV)]
        + [gate_spec(piece), gate_spec(piece)],
        out_shape=[shape_of((rows, w), BF) for w in sizes]
        + [shape_of((seqs * 8, w), F32) for w in sizes]
        + [shape_of((seqs, 8, w), F32) for w in sizes]
        + [shape_of((HEADS, 1, rows), F32)] * 2,
        scratch_shapes=held(piece, 8) + held(piece, 16),
        compiler_params=params(),
        cost_estimate=pl.CostEstimate(flops=45 * 10**9, bytes_accessed=30 * 2**20, transcendentals=0),
        name="close_rule",
    )(projected, projected, projected, edges, edges, edges, taps, taps, taps, betas, decays,
      inverse, states, incoming, grad, leaving)


SEQ = ("y", "x")
ALL = ("z", "c", "y", "x")


def product(left, right):
    return jnp.dot(left, right, preferred_element_type=F32)


def product_left(left, right):
    return lax.dot_general(left, right, (((0,), (0,)), ((), ())), preferred_element_type=F32)


def product_right(left, right):
    return lax.dot_general(left, right, (((1,), (1,)), ((), ())), preferred_element_type=F32)


def inverse_root(value):
    return lax.rsqrt(jnp.mean(value * value, axis=-1, keepdims=True) + EPS)


def norm_back(grad, normed, inverse, gain):
    scaled = grad * gain
    return (
        jnp.sum(grad * normed, axis=0),
        inverse * (scaled - normed * jnp.mean(scaled * normed, axis=-1, keepdims=True)),
    )


def shift(block, distance):
    devices = range(lax.axis_size(SEQ))
    return lax.ppermute(block, SEQ, [(i - distance, i) for i in devices if i - distance in devices])


def take(block, dim, index):
    return lax.dynamic_index_in_dim(block, index, dim, keepdims=False)


def tie(*values):
    return lax.optimization_barrier(values)


def partners(axis):
    size, me = lax.axis_size(axis), lax.axis_index(axis)
    if size & (size - 1):
        raise ValueError(f"{axis} has {size}")
    return [([(i, i ^ away) for i in range(size)], me ^ away) for away in range(1, size)]


class Sum:
    def __init__(self, parts):
        self.parts, self.left = parts, ["z", SEQ]
        self.sent_as = parts[0].dtype

    @classmethod
    def of_rows(cls, grad):
        shape = (lax.axis_size("z"), 2, lax.axis_size(SEQ), -1, grad.shape[1])
        whole, me = grad.reshape(shape), lax.axis_index("c")
        return cls([take(whole, 1, me), lax.ppermute(take(whole, 1, 1 - me), "c", [(0, 1), (1, 0)])])

    @classmethod
    def of_product(cls, halves, grad, extra=None):
        mine, other = halves
        outer, inner = lax.axis_size("z"), lax.axis_size(SEQ)

        def half(chosen, index):
            found = product_left(chosen, grad).astype(BF)
            if extra is not None:
                more = take(extra.reshape(outer, 2, -1, extra.shape[1]), 1, index)
                found = jnp.concatenate([found, more.reshape(-1, extra.shape[1])], axis=1)
            return found.reshape(outer, inner, -1, found.shape[1])

        me = lax.axis_index("c")
        sent = lax.ppermute(half(other, 1 - me), "c", [(0, 1), (1, 0)])
        return cls([half(mine, me), sent])

    def direct(self, axis):
        dim = self.left.index(axis)
        self.left.remove(axis)

        def share(index):
            return sum_of([take(part, dim, index) for part in self.parts]).astype(self.sent_as)

        came = [lax.ppermute(share(partner), axis, pairs) for pairs, partner in partners(axis)]
        self.parts = [share(lax.axis_index(axis))] + came
        return self

    def reduce(self, axis):
        dim = self.left.index(axis)
        self.left.remove(axis)
        total = jnp.moveaxis(sum_of(self.parts).astype(BF), dim, 0)
        folded = total.reshape(-1, total.shape[-1])
        folded = lax.psum_scatter(folded, axis, scatter_dimension=0, tiled=True)
        self.parts = [folded.reshape(total.shape[1:])]
        return self

    def tied(self, *values):
        out = tie(*values, *self.parts)
        self.parts = list(out[len(values) :])
        return out[0] if len(values) == 1 else out[: len(values)]

    def result(self):
        return sum_of(self.parts)


def core_halves(features):
    step = features.shape[1] // (2 * lax.axis_size("z"))
    firsts = jnp.concatenate([features[:, i : i + step] for i in range(0, features.shape[1], 2 * step)], axis=1)
    seconds = jnp.concatenate([features[:, i : i + step] for i in range(step, features.shape[1], 2 * step)], axis=1)
    me = lax.axis_index("c")
    return jnp.where(me == 0, firsts, seconds), jnp.where(me == 0, seconds, firsts)


def everywhere(total):
    for axis in ("c", "x", "y", "z"):
        size, away = lax.axis_size(axis), 1
        while away < size:
            total = total + lax.ppermute(total, axis, [(i, i ^ away) for i in range(size)])
            away *= 2
    return total


class Gather:
    def __init__(self, block):
        self.held, self.have, self.width = block, [], block.shape[-1]

    def along(self, axis):
        order = ("z", "c", SEQ)
        size, me, held = lax.axis_size(axis), lax.axis_index(axis), self.held
        dim = sum(order.index(other) < order.index(axis) for other in self.have)
        came = [lax.ppermute(held, axis, pairs) for pairs, _ in partners(axis)]
        entries = []
        for index in range(size):
            entry = held
            for away in range(1, size):
                entry = jnp.where(me == index ^ away, came[away - 1], entry)
            entries.append(entry)
        self.held = jnp.stack(entries, axis=dim)
        self.have.append(axis)
        return self

    def tied(self, value):
        value, self.held = tie(value, self.held)
        return value

    def result(self):
        return self.held.reshape(-1, self.width)


def sum_of(parts):
    total = parts[0].astype(F32)
    for part in parts[1:]:
        total = total + part.astype(F32)
    return total


def shards(
    tokens, cotangent, gain_mixer, proj_input, conv_filter, proj_gates, proj_outgate, gain_heads,
    proj_output, gain_feed, feed_gate, feed_up, feed_down, decay_log, decay_bias,
):
    seqs, piece = tokens.shape[0], tokens.shape[1]
    rows = seqs * piece
    width = HEADS * DK
    channels = 2 * width + HEADS * DV
    devices = lax.axis_size(ALL)
    own = proj_input.shape[0]

    extras = jnp.concatenate(
        [
            proj_gates,
            conv_filter.reshape(own, -1),
            gain_mixer[:, None],
            gain_feed[:, None],
            jnp.pad(gain_heads, (0, own - gain_heads.shape[0]))[:, None],
        ],
        axis=1,
    )
    extras = jnp.pad(extras, ((0, 0), (0, 128 - extras.shape[1])))
    group = lax.all_gather(jnp.concatenate([proj_input, extras], axis=1), ALL, axis=0, tiled=True)
    feed_group = lax.all_gather(jnp.concatenate([feed_gate, feed_up], axis=1), ALL, axis=0, tiled=True)
    all_outgate = Gather(proj_outgate).along("z").along(SEQ)
    all_output = Gather(proj_output).along("z")
    all_down = Gather(feed_down).along("z")
    group = all_down.tied(all_output.tied(all_outgate.tied(group)))
    all_outgate.along("c")
    all_output.along(SEQ)
    hidden_units = feed_gate.shape[1]

    input_matrix = group[:, :channels]
    small = group[:, channels:]
    gates_matrix = small[:, : 2 * HEADS]
    bank = small[:, 2 * HEADS : 2 * HEADS + 16].reshape(channels, CONV).astype(F32)
    gain_first = small[:, 2 * HEADS + 16].astype(F32)
    gain_second = small[:, 2 * HEADS + 17].astype(F32)
    heads_gain = small[:, 2 * HEADS + 18].reshape(devices, own)[:, : gain_heads.shape[0]].reshape(1, DV)
    heads_gain = jnp.broadcast_to(heads_gain.astype(F32), (8, DV))
    taps = jnp.pad(bank.T, ((0, 8 - CONV), (0, 0)))

    residual = tokens.astype(F32).reshape(rows, D)
    inverse_one = inverse_root(residual)
    normed_one = residual * inverse_one
    first = (normed_one * gain_first).astype(BF)
    projected = product(first, input_matrix).astype(BF)
    gate_pre = lax.dot_general(gates_matrix, first, (((0,), (1,)), ((), ())), preferred_element_type=F32)
    betas = jax.nn.sigmoid(gate_pre[:HEADS])
    decay_pre = gate_pre[HEADS:] + decay_bias[:, None]
    rates = jnp.exp(decay_log)[:, None]
    decays = -rates * jax.nn.softplus(decay_pre)
    beta_rows, decay_rows = betas.reshape(HEADS, 1, rows), decays.reshape(HEADS, 1, rows)
    edge = shift(projected.reshape(seqs, piece, channels)[:, piece - CONV + 1 :], 1)
    edges = jnp.pad(edge.astype(F32), ((0, 0), (9 - CONV, 0), (0, 0))).reshape(seqs * 8, channels)
    local, reading, states, inverse = open_rule(projected, edges, taps, beta_rows, decay_rows, seqs, piece)
    states = all_outgate.tied(all_output.tied(states))
    all_down.along(SEQ)
    outgate_matrix = all_outgate.result()
    outgate = product(first, outgate_matrix)
    all_output.along("c")

    pieces = lax.axis_size(SEQ)
    carried, transfer = states[:, :, -1, :, :DV], states[:, :, -1, :, DV:]
    incoming = jnp.zeros(carried.shape, BF)
    for hop in range(1, pieces):
        ending = carried.astype(F32) + jnp.einsum(
            "...dk,...ke->...de", transfer, incoming.astype(F32), precision=lax.Precision.HIGH
        )
        incoming = incoming + lax.ppermute(ending.astype(BF), SEQ, [(hop - 1, hop)])

    after = shift(transfer.astype(BF), -1)
    chains = [jnp.swapaxes(after, -1, -2)] if pieces > 2 else []
    for _ in range(pieces - 3):
        chain = jnp.einsum("...ki,...kj->...ij", after, shift(chains[-1], -1), preferred_element_type=F32)
        chains.append(chain.astype(BF))

    incoming = all_down.tied(all_output.tied(incoming))
    all_down.along("c")
    output_matrix = all_output.result()
    if chains:
        outgate, *chains = tie(outgate, *chains)
    mixed, gated = finish(local, reading, incoming, outgate, heads_gain, seqs, piece)
    middle = residual + product(gated, output_matrix)
    inverse_two = inverse_root(middle)
    normed_two = middle * inverse_two
    second = (normed_two * gain_second).astype(BF)
    gate_matrix, upward_matrix = feed_group[:, :hidden_units], feed_group[:, hidden_units:]
    down_matrix = all_down.result()
    up_gate = product(second, gate_matrix)
    up_linear = product(second, upward_matrix)
    sigmoid_gate = jax.nn.sigmoid(up_gate)
    silu_gate = up_gate * sigmoid_gate
    hidden = (silu_gate * up_linear).astype(BF)
    layer_out = (middle + product(hidden, down_matrix)).astype(BF)

    grad_branch = cotangent.reshape(rows, D)
    sum_down = Sum.of_rows(product_left(hidden, grad_branch).astype(BF))
    grad_hidden = product_right(grad_branch, down_matrix)
    grad_gate = (grad_hidden * up_linear * (sigmoid_gate + silu_gate * (1.0 - sigmoid_gate))).astype(BF)
    grad_up = (grad_hidden * silu_gate).astype(BF)
    sum_feed = Sum.of_product(core_halves(second), jnp.concatenate([grad_gate, grad_up], axis=1))
    grad_second = product_right(grad_gate, gate_matrix) + product_right(grad_up, upward_matrix)
    grad_second = sum_feed.tied(grad_second)
    sum_feed.reduce("z")
    grad_gain_feed, grad_norm_two = norm_back(grad_second, normed_two, inverse_two, gain_second)
    grad_middle = grad_branch.astype(F32) + grad_norm_two
    grad_mixer_out = grad_middle.astype(BF)
    grad_mixer_out = sum_down.tied(grad_mixer_out)
    sum_down.direct(SEQ)
    grad_gated = product_right(grad_mixer_out, output_matrix)
    grad_mixed, grad_outgate, gain_parts, flow = unfinish(
        grad_gated, mixed, outgate, heads_gain, reading, seqs, piece
    )
    grad_gain_heads = jnp.sum(gain_parts[:, :, 0], axis=(0, 1))

    flow = flow.astype(BF)
    leaving = shift(flow, -1).astype(F32)
    for ahead, chain in enumerate(chains, 2):
        leaving = leaving + jnp.einsum(
            "...ik,...ke->...ie", chain, shift(flow, -ahead), preferred_element_type=F32
        )
    first_halves = core_halves(first)
    sum_outgate = Sum.of_product(first_halves, grad_outgate)
    sum_output = Sum.of_rows(product_left(gated, grad_mixer_out).astype(BF))
    leaving = sum_feed.tied(sum_output.tied(sum_outgate.tied(sum_down.tied(leaving.astype(BF)))))
    sum_down.direct("z")
    sum_outgate.direct(SEQ)
    sum_output.direct(SEQ)
    sum_feed.reduce(SEQ)

    outs = close_rule(
        projected, edges, taps, beta_rows, decay_rows, inverse, states, incoming, grad_mixed, leaving, seqs, piece
    )
    outs = sum_outgate.tied(*sum_down.tied(*outs))
    sum_outgate.direct("z")
    grad_edges = jnp.concatenate(outs[3:6], axis=1).reshape(seqs, 8, channels)[:, 9 - CONV :]
    returned = shift(grad_edges.astype(BF), -1)
    starts = (0, width, 2 * width, channels)
    grad_parts = []
    for part, grad in enumerate(outs[:3]):
        back = returned[:, :, starts[part] : starts[part + 1]]
        grad = grad.reshape(seqs, piece, -1)
        tail = (grad[:, piece - 8 :].astype(F32) + jnp.pad(back.astype(F32), ((0, 0), (9 - CONV, 0), (0, 0)))).astype(BF)
        grad_parts.append(lax.dynamic_update_slice(grad, tail, (0, piece - 8, 0)).reshape(rows, -1))
    bank_grad = jnp.concatenate(outs[6:9], axis=2).sum(axis=0)[:CONV].T
    grad_betas, grad_decays = outs[9].reshape(HEADS, rows), outs[10].reshape(HEADS, rows)
    grad_beta_pre = grad_betas * betas * (1.0 - betas)
    grad_decay_pre = -rates * grad_decays * jax.nn.sigmoid(decay_pre)
    grad_decay_log = jnp.sum(grad_decays * decays, axis=1)
    grad_decay_bias = jnp.sum(grad_decay_pre, axis=1)
    grad_gates = jnp.concatenate([grad_beta_pre, grad_decay_pre], axis=0).astype(BF)
    grad_proj_gates = lax.dot_general(first, grad_gates, (((0,), (1,)), ((), ())), preferred_element_type=F32)

    packed_heads = jnp.pad(
        grad_gain_heads.reshape(devices, -1), ((0, 0), (0, own - gain_heads.shape[0]))
    ).reshape(D, 1)
    grad_extras = jnp.concatenate(
        [grad_proj_gates, bank_grad.reshape(D, 16), grad_gain_feed[:, None], packed_heads], axis=1
    )
    grad_extras = jnp.pad(grad_extras, ((0, 0), (0, 128 - grad_extras.shape[1]))).astype(BF)
    grad_query_key = jnp.concatenate(grad_parts[:2], axis=1)
    sum_query_key = Sum.of_product(first_halves, grad_query_key)
    sum_values = Sum.of_product(first_halves, grad_parts[2], grad_extras)
    grad_first = product_right(grad_outgate, outgate_matrix) + lax.dot_general(
        grad_gates, gates_matrix, (((0,), (1,)), ((), ())), preferred_element_type=F32
    )
    grad_first = sum_query_key.tied(sum_output.tied(grad_first))
    sum_query_key.direct("z")
    grad_first = grad_first + product_right(grad_parts[2], input_matrix[:, 2 * width :])
    grad_first = sum_values.tied(grad_first)
    sum_values.direct(SEQ)
    sum_output.direct("z")
    grad_first = grad_first + product_right(grad_query_key, input_matrix[:, : 2 * width])
    grad_gain_mixer, grad_norm_one = norm_back(grad_first, normed_one, inverse_one, gain_first)
    sum_gain = Sum.of_rows(grad_gain_mixer.reshape(devices, own))
    sum_gain.parts = list(sum_values.tied(*sum_gain.parts))
    sum_values.direct("z")
    sum_gain.direct(SEQ)
    sum_gain.parts = list(sum_query_key.tied(*sum_gain.parts))
    sum_query_key.direct(SEQ)
    sum_gain.direct("z")
    tokens_grad = (grad_middle + grad_norm_one).reshape(seqs, piece, D)
    sum_value_rows = sum_values.result()
    sum_proj_input = jnp.concatenate([sum_query_key.result(), sum_value_rows[:, : HEADS * DV]], axis=1)
    found_extras = sum_value_rows[:, HEADS * DV :]

    decay_sums = jnp.pad(jnp.stack([grad_decay_log, grad_decay_bias]), ((0, 6), (0, 128 - HEADS)))
    decay_sums = everywhere(decay_sums)
    feed_rows = sum_feed.result()
    return (
        layer_out.reshape(seqs, piece, D),
        tokens_grad,
        sum_gain.result().reshape(own),
        sum_proj_input,
        found_extras[:, 2 * HEADS : 2 * HEADS + 16].reshape(-1, CONV),
        found_extras[:, : 2 * HEADS],
        sum_outgate.result(),
        found_extras[: gain_heads.shape[0], 2 * HEADS + 17],
        sum_output.result(),
        found_extras[:, 2 * HEADS + 16],
        feed_rows[:, :hidden_units],
        feed_rows[:, hidden_units:],
        sum_down.result(),
        decay_sums[0, :HEADS],
        decay_sums[1, :HEADS],
    )


def solution(mesh):
    dp, seq = mesh.shape["dp"], mesh.shape["seq"]
    side = math.isqrt(seq)
    side = side if side * side == seq else 1
    fine = jax.sharding.Mesh(mesh.devices.reshape(dp // 2, 2, seq // side, side), ALL)
    row, vector, split = P(("z", "c"), SEQ, None), P(ALL), P(ALL, None)
    in_specs = (row, row, vector, split, split, split, split, vector, split, vector, split, split, split, P(), P())
    out_specs = (row, row, vector, split, split, split, split, vector, split, vector, split, split, split, P(), P())
    return jax.shard_map(shards, mesh=fine, in_specs=in_specs, out_specs=out_specs, check_vma=False)
```

```python
import functools
import math
import jax
import jax.numpy as jnp
from jax import lax
from jax.experimental import pallas as pl
from jax.experimental.pallas import tpu as pltpu
from jax.sharding import PartitionSpec as P

D = 1024
HEADS = 8
DK = 128
DV = 256
CONV = 4
CHUNK = 128
PAIR = 2
EPS = 1e-06
WIDE = DV + DK
VMEM = 56 * 1024 * 1024
BF = jnp.bfloat16
F32 = jnp.float32


def dot(left, right, over):
    return lax.dot_general(left, right, (((over[0],), (over[1],)), ((), ())), preferred_element_type=F32)


def split(value):
    if value.dtype == BF:
        return value, None
    high = value.astype(BF)
    return high, (value - high.astype(F32)).astype(BF)


def mm(left, right, over=(1, 0)):
    (left, left_low), (right, right_low) = split(left), split(right)
    total = dot(left, right, over)
    if left_low is not None:
        total = total + dot(left_low, right, over)
    if right_low is not None:
        total = total + dot(left, right_low, over)
    return total


def mm_nt(left, right):
    return mm(left, right, (1, 1))


def mm_tn(left, right):
    return mm(left, right, (0, 0))


def grids():
    rows = lax.broadcasted_iota(jnp.int32, (CHUNK, CHUNK), 0)
    cols = lax.broadcasted_iota(jnp.int32, (CHUNK, CHUNK), 1)
    return rows, cols


def to_column(row, rows, cols):
    return jnp.sum(jnp.where(rows == cols, row, 0.0), axis=1, keepdims=True)


def to_row(column, rows, cols):
    return jnp.sum(jnp.where(rows == cols, column, 0.0), axis=0, keepdims=True)


def fades(decay_row, beta_row, rows, cols):
    cumul = jnp.sum(jnp.where(cols <= rows, decay_row, 0.0), axis=1, keepdims=True)
    cumul_row = to_row(cumul, rows, cols)
    beta = to_column(beta_row, rows, cols)
    fading = jnp.exp(jnp.minimum(cumul - cumul_row, 0.0))
    strict = jnp.where(rows > cols, fading, 0.0)
    causal = jnp.where(rows >= cols, fading, 0.0)
    last = cumul[CHUNK - 1 : CHUNK]
    return beta, strict, causal, jnp.exp(cumul), jnp.exp(last - cumul), jnp.exp(last)


def unit_lower_inverses(lowers, rows, cols):
    def level(lower, width):
        shift = width.bit_length() - 1
        row_block, col_block = lax.shift_right_logical(rows, shift), lax.shift_right_logical(cols, shift)
        return jnp.where((row_block == col_block + 1) & ((col_block & 1) == 0), lower, 0.0)

    inverses = [jnp.where(rows == cols, 1.0, 0.0) - level(lower, 1) for lower in lowers]
    width = 2
    while width < CHUNK:
        steps = [mm(inverse, level(lower, width)) for inverse, lower in zip(inverses, lowers)]
        steps = [mm(step, inverse) for inverse, step in zip(inverses, steps)]
        inverses = [inverse - step for inverse, step in zip(inverses, steps)]
        width *= 2
    return inverses


def convolve(x, edge, taps, held, piece):
    held[0:8] = edge
    held[8 : 8 + piece] = x.astype(F32)
    total = taps[0:1] * held[5 : 5 + piece]
    for j in range(1, CONV):
        total = total + taps[j : j + 1] * held[5 + j : 5 + j + piece]
    return total


def units(active):
    inverse = lax.rsqrt(jnp.sum(active * active, axis=-1, keepdims=True) + EPS)
    return active * inverse, inverse


def opening_kernel(
    piece, q_ref, k_ref, v_ref, qe_ref, ke_ref, ve_ref, qf_ref, kf_ref, vf_ref, beta_ref, decay_ref,
    local_ref, reading_ref, states_ref, inverse_ref, held_q, held_k, held_v,
):
    rows, cols = grids()
    q_conv = convolve(q_ref[...], qe_ref[...], qf_ref[...], held_q, piece)
    k_conv = convolve(k_ref[...], ke_ref[...], kf_ref[...], held_k, piece)
    v_conv = convolve(v_ref[...], ve_ref[...], vf_ref[...], held_v, piece)
    q_act = q_conv * jax.nn.sigmoid(q_conv)
    k_act = k_conv * jax.nn.sigmoid(k_conv)
    v_act = v_conv * jax.nn.sigmoid(v_conv)
    chunks = piece // CHUNK
    parts = [slice(chunk * CHUNK, (chunk + 1) * CHUNK) for chunk in range(chunks)]
    terms = {}
    for head in range(PAIR):
        queries = units(q_act[:, head * DK : (head + 1) * DK])[0] * DK**-0.5
        keys = units(k_act[:, head * DK : (head + 1) * DK])[0]
        for chunk, part in enumerate(parts):
            query, key = queries[part], keys[part]
            beta, strict, causal, grow, fade, closing = fades(
                decay_ref[head, :, part], beta_ref[head, :, part], rows, cols
            )
            both = mm_nt(jnp.concatenate([key, query], axis=0), key)
            value = beta * v_act[part, head * DV : (head + 1) * DV]
            terms[head, chunk] = (
                beta * both[:CHUNK] * strict,
                both[CHUNK:] * causal,
                jnp.concatenate([key * (beta * grow), query * grow], axis=0),
                key * fade,
                jnp.concatenate([value, jnp.zeros((CHUNK, DK), F32)], axis=1),
                closing,
            )
    inverses = unit_lower_inverses([term[0] for term in terms.values()], rows, cols)
    inverses = dict(zip(terms, inverses))
    opening = jnp.concatenate([jnp.zeros((DK, DV), F32), jnp.where(rows == cols, 1.0, 0.0)], axis=1)
    held_states = [opening] * PAIR
    for chunk, part in enumerate(parts):
        for head in range(PAIR):
            _, scores, looking, tail, value, closing = terms[head, chunk]
            inverse, state = inverses[head, chunk], held_states[head]
            inverse_ref[part, head * CHUNK : (head + 1) * CHUNK] = inverse
            seen = mm(looking, state)
            fresh = mm(inverse, value - seen[:CHUNK])
            result = seen[CHUNK:] + mm(scores, fresh)
            state = closing * state + mm_tn(tail, fresh)
            held_states[head] = state
            local_ref[part, head * DV : (head + 1) * DV] = result[:, :DV]
            reading_ref[part, head * DK : (head + 1) * DK] = result[:, DV:]
            states_ref[0, head, chunk] = state


def finish_kernel(local_ref, reading_ref, incoming_ref, outgate_ref, gain_ref, mixed_ref, gated_ref):
    for head in range(PAIR):
        wide = slice(head * DV, (head + 1) * DV)
        mixed = local_ref[:, wide] + mm(reading_ref[:, head * DK : (head + 1) * DK], incoming_ref[0, head])
        mixed_ref[:, wide] = mixed
        inverse = lax.rsqrt(jnp.mean(mixed * mixed, axis=-1, keepdims=True) + EPS)
        outgate = outgate_ref[:, wide]
        gated = mixed * inverse * gain_ref[0:1] * (outgate * jax.nn.sigmoid(outgate))
        gated_ref[:, wide] = gated.astype(BF)


def unfinish_kernel(
    grad_ref, mixed_ref, outgate_ref, gain_ref, reading_ref, grad_mixed_ref, grad_outgate_ref, gain_grad_ref, flow_ref
):
    gain = gain_ref[0:1]
    for head in range(PAIR):
        wide = slice(head * DV, (head + 1) * DV)
        mixed, outgate, grad = mixed_ref[:, wide], outgate_ref[:, wide], grad_ref[:, wide]
        inverse = lax.rsqrt(jnp.mean(mixed * mixed, axis=-1, keepdims=True) + EPS)
        normed = mixed * inverse
        sigmoid = jax.nn.sigmoid(outgate)
        gate = outgate * sigmoid
        along = grad * normed
        gain_grad = jnp.sum(along * gate, axis=0, keepdims=True)
        gain_grad_ref[0, head] = jnp.broadcast_to(gain_grad, (8, DV))
        grad_outgate_ref[:, wide] = (along * gain * (sigmoid + gate * (1.0 - sigmoid))).astype(BF)
        scaled = grad * gain * gate
        grad_mixed = inverse * (scaled - normed * jnp.mean(scaled * normed, axis=-1, keepdims=True))
        grad_mixed_ref[:, wide] = grad_mixed
        flow_ref[0, head] = mm_tn(reading_ref[:, head * DK : (head + 1) * DK], grad_mixed)


def unconvolve(grad, taps, held_in, held_out, piece, grad_ref, edge_ref, taps_ref):
    width = grad.shape[1]
    held_out[0:8] = jnp.zeros((8, width), F32)
    held_out[8 : 8 + piece] = grad
    held_out[8 + piece : 16 + piece] = jnp.zeros((8, width), F32)
    total = taps[0:1] * held_out[11 : 11 + piece]
    edge = taps[0:1] * held_out[3:11]
    for j in range(1, CONV):
        total = total + taps[j : j + 1] * held_out[11 - j : 11 - j + piece]
        edge = edge + taps[j : j + 1] * held_out[3 - j : 11 - j]
    grad_ref[...] = total.astype(BF)
    edge_ref[...] = edge
    sums = [jnp.sum(grad * held_in[5 + j : 5 + j + piece], axis=0, keepdims=True) for j in range(CONV)]
    taps_ref[0] = jnp.concatenate(sums + [jnp.zeros((8 - CONV, width), F32)], axis=0)


def silu_slope(value, sigmoid):
    return sigmoid * (1.0 + value * (1.0 - sigmoid))


def closing_kernel(
    piece, q_ref, k_ref, v_ref, qe_ref, ke_ref, ve_ref, qf_ref, kf_ref, vf_ref, beta_ref, decay_ref,
    inverse_ref, states_ref, incoming_ref, grad_ref, leaving_ref,
    dq_ref, dk_ref, dv_ref, dqe_ref, dke_ref, dve_ref, dqf_ref, dkf_ref, dvf_ref, dbeta_ref, ddecay_ref,
    held_q, held_k, held_v, back_q, back_k, back_v,
):
    rows, cols = grids()
    q_conv = convolve(q_ref[...], qe_ref[...], qf_ref[...], held_q, piece)
    k_conv = convolve(k_ref[...], ke_ref[...], kf_ref[...], held_k, piece)
    v_conv = convolve(v_ref[...], ve_ref[...], vf_ref[...], held_v, piece)
    q_sig, k_sig, v_sig = jax.nn.sigmoid(q_conv), jax.nn.sigmoid(k_conv), jax.nn.sigmoid(v_conv)
    q_act, k_act, v_act = q_conv * q_sig, k_conv * k_sig, v_conv * v_sig
    chunks = piece // CHUNK
    parts = [slice(chunk * CHUNK, (chunk + 1) * CHUNK) for chunk in range(chunks)]
    narrows = [slice(head * DK, (head + 1) * DK) for head in range(PAIR)]
    wides = [slice(head * DV, (head + 1) * DV) for head in range(PAIR)]
    places = [(head, chunk) for chunk in reversed(range(chunks)) for head in range(PAIR)]
    unit_parts = [units(q_act[:, narrow]) + units(k_act[:, narrow]) for narrow in narrows]
    terms = {}
    for head, chunk in places:
        part = parts[chunk]
        query, key = unit_parts[head][0][part] * DK**-0.5, unit_parts[head][2][part]
        beta, strict, causal, grow, fade, closing = fades(
            decay_ref[head, :, part], beta_ref[head, :, part], rows, cols
        )
        both = mm_nt(jnp.concatenate([key, query], axis=0), key)
        scores = both[CHUNK:] * causal
        incoming = incoming_ref[0, head]
        if chunk == 0:
            state = incoming.astype(F32)
        else:
            before = states_ref[0, head, chunk - 1]
            state = before[:, :DV] + mm(before[:, DV:], incoming)
        seen = mm(key, state)
        grad = grad_ref[part, wides[head]]
        terms[head, chunk] = dict(
            query=query, key=key, beta=beta, strict=strict, causal=causal, grow=grow, fade=fade, closing=closing,
            cross=both[:CHUNK] * strict, scores=scores, state=state, seen=seen, grad=grad,
            plain=v_act[part, wides[head]] - grow * seen,
            inverse=inverse_ref[part, head * CHUNK : (head + 1) * CHUNK],
            grad_fresh=mm_tn(scores, grad), grad_state=mm_tn(query * grow, grad),
        )
    for place in places:
        term = terms[place]
        term["fresh"] = mm(term["inverse"], term["beta"] * term["plain"])
    grad_states = [leaving_ref[0, head].astype(F32) for head in range(PAIR)]
    for place in places:
        term, grad_state = terms[place], grad_states[place[0]]
        key = term["key"]
        grad_fresh = term["grad_fresh"] + mm(key * term["fade"], grad_state)
        grad_right = mm_tn(term["inverse"], grad_fresh)
        term["grad_right"], term["grad_seen"] = grad_right, -(term["beta"] * term["grow"]) * grad_right
        term["grad_after"] = grad_state
        grad_states[place[0]] = term["closing"] * grad_state + term["grad_state"] + mm_tn(key, term["grad_seen"])
    for head, chunk in places:
        term, part = terms[head, chunk], parts[chunk]
        query, key, beta, strict, causal, grow, fade, closing, cross, scores, state, seen, grad = [
            term[name]
            for name in (
                "query", "key", "beta", "strict", "causal", "grow", "fade", "closing", "cross", "scores", "state",
                "seen", "grad",
            )
        ]
        grad_right, grad_seen, grad_state, fresh = [
            term[name] for name in ("grad_right", "grad_seen", "grad_after", "fresh")
        ]
        pair = mm_nt(jnp.concatenate([grad, grad_right], axis=0), fresh)
        grad_scores = jnp.where(rows >= cols, pair[:CHUNK], 0.0)
        grad_lower = jnp.where(rows > cols, -pair[CHUNK:], 0.0)
        pair = mm_nt(jnp.concatenate([grad, grad_seen], axis=0), state)
        grad_lifted, grad_key = pair[:CHUNK], pair[CHUNK:]
        grad_tail = mm_nt(fresh, grad_state)
        grad_cross = grad_lower * strict * beta
        grad_both = grad_scores * causal
        term["grad_query"] = mm(grad_both, key) + grad_lifted * grow
        term["grad_key"] = (
            grad_key
            + mm(grad_cross, key)
            + mm_tn(jnp.concatenate([grad_cross, grad_both], axis=0), jnp.concatenate([key, query], axis=0))
            + grad_tail * fade
        )
        spread = grad_lower * beta * cross + grad_scores * scores
        tail_sum = jnp.sum(grad_tail * (key * fade), axis=1, keepdims=True)
        grad_cumul = (
            jnp.sum(spread, axis=1, keepdims=True)
            - to_column(jnp.sum(spread, axis=0, keepdims=True), rows, cols)
            + jnp.sum(grad_lifted * (query * grow) - grad_tail * (key * fade), axis=1, keepdims=True)
            + jnp.sum(grad_seen * seen, axis=1, keepdims=True)
        )
        grad_last = jnp.sum(tail_sum, axis=0, keepdims=True) + closing * jnp.sum(
            jnp.sum(state * grad_state, axis=0, keepdims=True), axis=1, keepdims=True
        )
        ddecay_ref[head, :, part] = (
            jnp.sum(jnp.where(rows >= cols, grad_cumul, 0.0), axis=0, keepdims=True) + grad_last
        )
        grad_beta = jnp.sum(grad_right * term["plain"], axis=1, keepdims=True) + jnp.sum(
            grad_lower * cross, axis=1, keepdims=True
        )
        dbeta_ref[head, :, part] = to_row(grad_beta, rows, cols)
    dq_all, dk_all, dv_all = [], [], []
    for head in range(PAIR):
        query_unit, query_scale, keys, key_scale = unit_parts[head]
        dq, dk = [
            jnp.concatenate([terms[head, chunk][name] for chunk in range(chunks)], axis=0)
            for name in ("grad_query", "grad_key")
        ]
        dq = dq * DK**-0.5
        dq_all.append(query_scale * (dq - query_unit * jnp.sum(dq * query_unit, axis=-1, keepdims=True)))
        dk_all.append(key_scale * (dk - keys * jnp.sum(dk * keys, axis=-1, keepdims=True)))
        dv_all.append(
            jnp.concatenate(
                [terms[head, chunk]["beta"] * terms[head, chunk]["grad_right"] for chunk in range(chunks)], axis=0
            )
        )
    dq = jnp.concatenate(dq_all, axis=1) * silu_slope(q_conv, q_sig)
    dk = jnp.concatenate(dk_all, axis=1) * silu_slope(k_conv, k_sig)
    dv = jnp.concatenate(dv_all, axis=1) * silu_slope(v_conv, v_sig)
    unconvolve(dq, qf_ref[...], held_q, back_q, piece, dq_ref, dqe_ref, dqf_ref)
    unconvolve(dk, kf_ref[...], held_k, back_k, piece, dk_ref, dke_ref, dkf_ref)
    unconvolve(dv, vf_ref[...], held_v, back_v, piece, dv_ref, dve_ref, dvf_ref)


def column_specs(rows, first_axis):
    steps = HEADS // PAIR
    return [
        pl.BlockSpec((rows, PAIR * DK), lambda h, s: (s if first_axis else 0, h)),
        pl.BlockSpec((rows, PAIR * DK), lambda h, s: (s if first_axis else 0, steps + h)),
        pl.BlockSpec((rows, PAIR * DV), lambda h, s: (s if first_axis else 0, steps + h)),
    ]


def gate_spec(piece):
    return pl.BlockSpec((PAIR, 1, piece), lambda h, s: (h, 0, s))


def rows_spec(piece, width):
    return pl.BlockSpec((piece, PAIR * width), lambda h, s: (s, h))


def head_spec(*shape):
    zeros = (0,) * len(shape)
    return pl.BlockSpec((1, PAIR) + shape, lambda h, s: (s, h) + zeros)


def params():
    return pltpu.CompilerParams(vmem_limit_bytes=VMEM, dimension_semantics=("arbitrary", "arbitrary"))


def shape_of(shape, dtype):
    return jax.ShapeDtypeStruct(shape, dtype)


def held(piece, extra):
    return [pltpu.VMEM((piece + extra, PAIR * width), F32) for width in (DK, DK, DV)]


def open_rule(projected, edges, taps, betas, decays, seqs, piece):
    rows, chunks = seqs * piece, piece // CHUNK
    return pl.pallas_call(
        functools.partial(opening_kernel, piece),
        grid=(HEADS // PAIR, seqs),
        in_specs=column_specs(piece, True) + column_specs(8, True) + column_specs(8, False)
        + [gate_spec(piece), gate_spec(piece)],
        out_specs=[rows_spec(piece, DV), rows_spec(piece, DK), head_spec(chunks, DK, WIDE), rows_spec(piece, CHUNK)],
        out_shape=[
            shape_of((rows, HEADS * DV), F32),
            shape_of((rows, HEADS * DK), F32),
            shape_of((seqs, HEADS, chunks, DK, WIDE), F32),
            shape_of((rows, HEADS * CHUNK), F32),
        ],
        scratch_shapes=held(piece, 8),
        compiler_params=params(),
        cost_estimate=pl.CostEstimate(flops=30 * 10**9, bytes_accessed=20 * 2**20, transcendentals=0),
        name="open_rule",
    )(projected, projected, projected, edges, edges, edges, taps, taps, taps, betas, decays)


def finish(local, reading, incoming, outgate, gain, seqs, piece):
    rows = seqs * piece
    return pl.pallas_call(
        finish_kernel,
        grid=(HEADS // PAIR, seqs),
        in_specs=[
            rows_spec(piece, DV), rows_spec(piece, DK), head_spec(DK, DV), rows_spec(piece, DV),
            pl.BlockSpec((8, DV), lambda h, s: (0, 0)),
        ],
        out_specs=[rows_spec(piece, DV), rows_spec(piece, DV)],
        out_shape=[shape_of((rows, HEADS * DV), F32), shape_of((rows, HEADS * DV), BF)],
        compiler_params=params(),
        name="finish_heads",
    )(local, reading, incoming, outgate, gain)


def unfinish(grad, mixed, outgate, gain, reading, seqs, piece):
    rows = seqs * piece
    return pl.pallas_call(
        unfinish_kernel,
        grid=(HEADS // PAIR, seqs),
        in_specs=[
            rows_spec(piece, DV), rows_spec(piece, DV), rows_spec(piece, DV),
            pl.BlockSpec((8, DV), lambda h, s: (0, 0)), rows_spec(piece, DK),
        ],
        out_specs=[rows_spec(piece, DV), rows_spec(piece, DV), head_spec(8, DV), head_spec(DK, DV)],
        out_shape=[
            shape_of((rows, HEADS * DV), F32), shape_of((rows, HEADS * DV), BF),
            shape_of((seqs, HEADS, 8, DV), F32), shape_of((seqs, HEADS, DK, DV), F32),
        ],
        compiler_params=params(),
        name="unfinish_heads",
    )(grad, mixed, outgate, gain, reading)


def close_rule(projected, edges, taps, betas, decays, inverse, states, incoming, grad, leaving, seqs, piece):
    rows, chunks = seqs * piece, piece // CHUNK
    sizes = (HEADS * DK, HEADS * DK, HEADS * DV)
    steps = HEADS // PAIR

    def blocks(height):
        return [pl.BlockSpec((height, PAIR * w), lambda h, s: (s, h)) for w in (DK, DK, DV)]

    return pl.pallas_call(
        functools.partial(closing_kernel, piece),
        grid=(steps, seqs),
        in_specs=column_specs(piece, True) + column_specs(8, True) + column_specs(8, False)
        + [gate_spec(piece), gate_spec(piece), rows_spec(piece, CHUNK), head_spec(chunks, DK, WIDE),
           head_spec(DK, DV), rows_spec(piece, DV), head_spec(DK, DV)],
        out_specs=blocks(piece) + blocks(8)
        + [pl.BlockSpec((1, 8, PAIR * w), lambda h, s: (s, 0, h)) for w in (DK, DK, DV)]
        + [gate_spec(piece), gate_spec(piece)],
        out_shape=[shape_of((rows, w), BF) for w in sizes]
        + [shape_of((seqs * 8, w), F32) for w in sizes]
        + [shape_of((seqs, 8, w), F32) for w in sizes]
        + [shape_of((HEADS, 1, rows), F32)] * 2,
        scratch_shapes=held(piece, 8) + held(piece, 16),
        compiler_params=params(),
        cost_estimate=pl.CostEstimate(flops=45 * 10**9, bytes_accessed=30 * 2**20, transcendentals=0),
        name="close_rule",
    )(projected, projected, projected, edges, edges, edges, taps, taps, taps, betas, decays,
      inverse, states, incoming, grad, leaving)


SEQ = ("y", "x")
ALL = ("z", "c", "y", "x")


def product(left, right):
    return jnp.dot(left, right, preferred_element_type=F32)


def product_left(left, right):
    return lax.dot_general(left, right, (((0,), (0,)), ((), ())), preferred_element_type=F32)


def product_right(left, right):
    return lax.dot_general(left, right, (((1,), (1,)), ((), ())), preferred_element_type=F32)


def inverse_root(value):
    return lax.rsqrt(jnp.mean(value * value, axis=-1, keepdims=True) + EPS)


def norm_back(grad, normed, inverse, gain):
    scaled = grad * gain
    return (
        jnp.sum(grad * normed, axis=0),
        inverse * (scaled - normed * jnp.mean(scaled * normed, axis=-1, keepdims=True)),
    )


def shift(block, distance):
    devices = range(lax.axis_size(SEQ))
    return lax.ppermute(block, SEQ, [(i - distance, i) for i in devices if i - distance in devices])


def take(block, dim, index):
    return lax.dynamic_index_in_dim(block, index, dim, keepdims=False)


def tie(*values):
    return lax.optimization_barrier(values)


def partners(axis):
    size, me = lax.axis_size(axis), lax.axis_index(axis)
    if size & (size - 1):
        raise ValueError(f"{axis} has {size}")
    return [([(i, i ^ away) for i in range(size)], me ^ away) for away in range(1, size)]


class Sum:
    def __init__(self, parts):
        self.parts, self.left = parts, ["z", SEQ]
        self.sent_as = parts[0].dtype

    @classmethod
    def of_rows(cls, grad):
        shape = (lax.axis_size("z"), 2, lax.axis_size(SEQ), -1, grad.shape[1])
        whole, me = grad.reshape(shape), lax.axis_index("c")
        return cls([take(whole, 1, me), lax.ppermute(take(whole, 1, 1 - me), "c", [(0, 1), (1, 0)])])

    @classmethod
    def of_product(cls, halves, grad, extra=None):
        mine, other = halves
        outer, inner = lax.axis_size("z"), lax.axis_size(SEQ)

        def half(chosen, index):
            found = product_left(chosen, grad).astype(BF)
            if extra is not None:
                more = take(extra.reshape(outer, 2, -1, extra.shape[1]), 1, index)
                found = jnp.concatenate([found, more.reshape(-1, extra.shape[1])], axis=1)
            return found.reshape(outer, inner, -1, found.shape[1])

        me = lax.axis_index("c")
        sent = lax.ppermute(half(other, 1 - me), "c", [(0, 1), (1, 0)])
        return cls([half(mine, me), sent])

    def direct(self, axis):
        dim = self.left.index(axis)
        self.left.remove(axis)

        def share(index):
            return sum_of([take(part, dim, index) for part in self.parts]).astype(self.sent_as)

        came = [lax.ppermute(share(partner), axis, pairs) for pairs, partner in partners(axis)]
        self.parts = [share(lax.axis_index(axis))] + came
        return self

    def reduce(self, axis):
        dim = self.left.index(axis)
        self.left.remove(axis)
        total = jnp.moveaxis(sum_of(self.parts).astype(BF), dim, 0)
        folded = total.reshape(-1, total.shape[-1])
        folded = lax.psum_scatter(folded, axis, scatter_dimension=0, tiled=True)
        self.parts = [folded.reshape(total.shape[1:])]
        return self

    def tied(self, *values):
        out = tie(*values, *self.parts)
        self.parts = list(out[len(values) :])
        return out[0] if len(values) == 1 else out[: len(values)]

    def result(self):
        return sum_of(self.parts)


def core_halves(features):
    step = features.shape[1] // (2 * lax.axis_size("z"))
    firsts = jnp.concatenate([features[:, i : i + step] for i in range(0, features.shape[1], 2 * step)], axis=1)
    seconds = jnp.concatenate([features[:, i : i + step] for i in range(step, features.shape[1], 2 * step)], axis=1)
    me = lax.axis_index("c")
    return jnp.where(me == 0, firsts, seconds), jnp.where(me == 0, seconds, firsts)


def everywhere(total):
    for axis in ("c", "x", "y", "z"):
        size, away = lax.axis_size(axis), 1
        while away < size:
            total = total + lax.ppermute(total, axis, [(i, i ^ away) for i in range(size)])
            away *= 2
    return total


class Gather:
    def __init__(self, block):
        self.held, self.have, self.width = block, [], block.shape[-1]

    def along(self, axis):
        order = ("z", "c", SEQ)
        size, me, held = lax.axis_size(axis), lax.axis_index(axis), self.held
        dim = sum(order.index(other) < order.index(axis) for other in self.have)
        came = [lax.ppermute(held, axis, pairs) for pairs, _ in partners(axis)]
        entries = []
        for index in range(size):
            entry = held
            for away in range(1, size):
                entry = jnp.where(me == index ^ away, came[away - 1], entry)
            entries.append(entry)
        self.held = jnp.stack(entries, axis=dim)
        self.have.append(axis)
        return self

    def tied(self, value):
        value, self.held = tie(value, self.held)
        return value

    def result(self):
        return self.held.reshape(-1, self.width)


def sum_of(parts):
    total = parts[0].astype(F32)
    for part in parts[1:]:
        total = total + part.astype(F32)
    return total


def shards(
    tokens, cotangent, gain_mixer, proj_input, conv_filter, proj_gates, proj_outgate, gain_heads,
    proj_output, gain_feed, feed_gate, feed_up, feed_down, decay_log, decay_bias,
):
    seqs, piece = tokens.shape[0], tokens.shape[1]
    rows = seqs * piece
    width = HEADS * DK
    channels = 2 * width + HEADS * DV
    devices = lax.axis_size(ALL)
    own = proj_input.shape[0]

    extras = jnp.concatenate(
        [
            proj_gates,
            conv_filter.reshape(own, -1),
            gain_mixer[:, None],
            gain_feed[:, None],
            jnp.pad(gain_heads, (0, own - gain_heads.shape[0]))[:, None],
        ],
        axis=1,
    )
    extras = jnp.pad(extras, ((0, 0), (0, 128 - extras.shape[1])))
    group = lax.all_gather(jnp.concatenate([proj_input, extras], axis=1), ALL, axis=0, tiled=True)
    feed_group = lax.all_gather(jnp.concatenate([feed_gate, feed_up], axis=1), ALL, axis=0, tiled=True)
    all_outgate = Gather(proj_outgate).along("z").along(SEQ)
    all_output = Gather(proj_output).along("z")
    all_down = Gather(feed_down).along("z")
    group = all_down.tied(all_output.tied(all_outgate.tied(group)))
    all_outgate.along("c")
    all_output.along(SEQ)
    hidden_units = feed_gate.shape[1]

    input_matrix = group[:, :channels]
    small = group[:, channels:]
    gates_matrix = small[:, : 2 * HEADS]
    bank = small[:, 2 * HEADS : 2 * HEADS + 16].reshape(channels, CONV).astype(F32)
    gain_first = small[:, 2 * HEADS + 16].astype(F32)
    gain_second = small[:, 2 * HEADS + 17].astype(F32)
    heads_gain = small[:, 2 * HEADS + 18].reshape(devices, own)[:, : gain_heads.shape[0]].reshape(1, DV)
    heads_gain = jnp.broadcast_to(heads_gain.astype(F32), (8, DV))
    taps = jnp.pad(bank.T, ((0, 8 - CONV), (0, 0)))

    residual = tokens.astype(F32).reshape(rows, D)
    inverse_one = inverse_root(residual)
    normed_one = residual * inverse_one
    first = (normed_one * gain_first).astype(BF)
    projected = product(first, input_matrix).astype(BF)
    gate_pre = lax.dot_general(gates_matrix, first, (((0,), (1,)), ((), ())), preferred_element_type=F32)
    betas = jax.nn.sigmoid(gate_pre[:HEADS])
    decay_pre = gate_pre[HEADS:] + decay_bias[:, None]
    rates = jnp.exp(decay_log)[:, None]
    decays = -rates * jax.nn.softplus(decay_pre)
    beta_rows, decay_rows = betas.reshape(HEADS, 1, rows), decays.reshape(HEADS, 1, rows)
    edge = shift(projected.reshape(seqs, piece, channels)[:, piece - CONV + 1 :], 1)
    edges = jnp.pad(edge.astype(F32), ((0, 0), (9 - CONV, 0), (0, 0))).reshape(seqs * 8, channels)
    local, reading, states, inverse = open_rule(projected, edges, taps, beta_rows, decay_rows, seqs, piece)
    states = all_outgate.tied(all_output.tied(states))
    all_down.along(SEQ)
    outgate_matrix = all_outgate.result()
    outgate = product(first, outgate_matrix)
    all_output.along("c")

    pieces = lax.axis_size(SEQ)
    carried, transfer = states[:, :, -1, :, :DV], states[:, :, -1, :, DV:]
    incoming = jnp.zeros(carried.shape, BF)
    for hop in range(1, pieces):
        ending = carried.astype(F32) + jnp.einsum(
            "...dk,...ke->...de", transfer, incoming.astype(F32), precision=lax.Precision.HIGH
        )
        incoming = incoming + lax.ppermute(ending.astype(BF), SEQ, [(hop - 1, hop)])

    after = shift(transfer.astype(BF), -1)
    chains = [jnp.swapaxes(after, -1, -2)] if pieces > 2 else []
    for _ in range(pieces - 3):
        chain = jnp.einsum("...ki,...kj->...ij", after, shift(chains[-1], -1), preferred_element_type=F32)
        chains.append(chain.astype(BF))

    incoming = all_down.tied(all_output.tied(incoming))
    all_down.along("c")
    output_matrix = all_output.result()
    if chains:
        outgate, *chains = tie(outgate, *chains)
    mixed, gated = finish(local, reading, incoming, outgate, heads_gain, seqs, piece)
    middle = residual + product(gated, output_matrix)
    inverse_two = inverse_root(middle)
    normed_two = middle * inverse_two
    second = (normed_two * gain_second).astype(BF)
    gate_matrix, upward_matrix = feed_group[:, :hidden_units], feed_group[:, hidden_units:]
    down_matrix = all_down.result()
    up_gate = product(second, gate_matrix)
    up_linear = product(second, upward_matrix)
    sigmoid_gate = jax.nn.sigmoid(up_gate)
    silu_gate = up_gate * sigmoid_gate
    hidden = (silu_gate * up_linear).astype(BF)
    layer_out = (middle + product(hidden, down_matrix)).astype(BF)

    grad_branch = cotangent.reshape(rows, D)
    sum_down = Sum.of_rows(product_left(hidden, grad_branch).astype(BF))
    grad_hidden = product_right(grad_branch, down_matrix)
    grad_gate = (grad_hidden * up_linear * (sigmoid_gate + silu_gate * (1.0 - sigmoid_gate))).astype(BF)
    grad_up = (grad_hidden * silu_gate).astype(BF)
    sum_feed = Sum.of_product(core_halves(second), jnp.concatenate([grad_gate, grad_up], axis=1))
    grad_second = product_right(grad_gate, gate_matrix) + product_right(grad_up, upward_matrix)
    grad_second = sum_feed.tied(grad_second)
    sum_feed.reduce("z")
    grad_gain_feed, grad_norm_two = norm_back(grad_second, normed_two, inverse_two, gain_second)
    grad_middle = grad_branch.astype(F32) + grad_norm_two
    grad_mixer_out = grad_middle.astype(BF)
    grad_gated = product_right(grad_mixer_out, output_matrix)
    grad_mixed, grad_outgate, gain_parts, flow = unfinish(
        grad_gated, mixed, outgate, heads_gain, reading, seqs, piece
    )
    grad_gain_heads = jnp.sum(gain_parts[:, :, 0], axis=(0, 1))

    flow = flow.astype(BF)
    leaving = shift(flow, -1).astype(F32)
    for ahead, chain in enumerate(chains, 2):
        leaving = leaving + jnp.einsum(
            "...ik,...ke->...ie", chain, shift(flow, -ahead), preferred_element_type=F32
        )
    first_halves = core_halves(first)
    sum_outgate = Sum.of_product(first_halves, grad_outgate)
    sum_output = Sum.of_rows(product_left(gated, grad_mixer_out).astype(BF))
    leaving = sum_feed.tied(sum_output.tied(sum_outgate.tied(sum_down.tied(leaving.astype(BF)))))
    sum_down.direct(SEQ)
    sum_outgate.direct(SEQ)
    sum_output.direct(SEQ)
    sum_feed.reduce(SEQ)

    outs = close_rule(
        projected, edges, taps, beta_rows, decay_rows, inverse, states, incoming, grad_mixed, leaving, seqs, piece
    )
    outs = sum_outgate.tied(*sum_down.tied(*outs))
    sum_down.direct("z")
    sum_outgate.direct("z")
    grad_edges = jnp.concatenate(outs[3:6], axis=1).reshape(seqs, 8, channels)[:, 9 - CONV :]
    returned = shift(grad_edges.astype(BF), -1)
    starts = (0, width, 2 * width, channels)
    grad_parts = []
    for part, grad in enumerate(outs[:3]):
        back = returned[:, :, starts[part] : starts[part + 1]]
        grad = grad.reshape(seqs, piece, -1)
        tail = (grad[:, piece - 8 :].astype(F32) + jnp.pad(back.astype(F32), ((0, 0), (9 - CONV, 0), (0, 0)))).astype(BF)
        grad_parts.append(lax.dynamic_update_slice(grad, tail, (0, piece - 8, 0)).reshape(rows, -1))
    bank_grad = jnp.concatenate(outs[6:9], axis=2).sum(axis=0)[:CONV].T
    grad_betas, grad_decays = outs[9].reshape(HEADS, rows), outs[10].reshape(HEADS, rows)
    grad_beta_pre = grad_betas * betas * (1.0 - betas)
    grad_decay_pre = -rates * grad_decays * jax.nn.sigmoid(decay_pre)
    grad_decay_log = jnp.sum(grad_decays * decays, axis=1)
    grad_decay_bias = jnp.sum(grad_decay_pre, axis=1)
    grad_gates = jnp.concatenate([grad_beta_pre, grad_decay_pre], axis=0).astype(BF)
    grad_proj_gates = lax.dot_general(first, grad_gates, (((0,), (1,)), ((), ())), preferred_element_type=F32)

    packed_heads = jnp.pad(
        grad_gain_heads.reshape(devices, -1), ((0, 0), (0, own - gain_heads.shape[0]))
    ).reshape(D, 1)
    grad_extras = jnp.concatenate(
        [grad_proj_gates, bank_grad.reshape(D, 16), grad_gain_feed[:, None], packed_heads], axis=1
    )
    grad_extras = jnp.pad(grad_extras, ((0, 0), (0, 128 - grad_extras.shape[1]))).astype(BF)
    grad_query_key = jnp.concatenate(grad_parts[:2], axis=1)
    sum_query_key = Sum.of_product(first_halves, grad_query_key)
    sum_values = Sum.of_product(first_halves, grad_parts[2], grad_extras)
    grad_first = product_right(grad_outgate, outgate_matrix) + lax.dot_general(
        grad_gates, gates_matrix, (((0,), (1,)), ((), ())), preferred_element_type=F32
    )
    grad_first = sum_query_key.tied(sum_output.tied(grad_first))
    sum_query_key.direct("z")
    grad_first = grad_first + product_right(grad_parts[2], input_matrix[:, 2 * width :])
    grad_first = sum_values.tied(grad_first)
    sum_values.direct(SEQ)
    sum_output.direct("z")
    grad_first = grad_first + product_right(grad_query_key, input_matrix[:, : 2 * width])
    grad_gain_mixer, grad_norm_one = norm_back(grad_first, normed_one, inverse_one, gain_first)
    sum_gain = Sum.of_rows(grad_gain_mixer.reshape(devices, own))
    sum_gain.parts = list(sum_values.tied(*sum_gain.parts))
    sum_values.direct("z")
    sum_gain.direct(SEQ)
    sum_gain.parts = list(sum_query_key.tied(*sum_gain.parts))
    sum_query_key.direct(SEQ)
    sum_gain.direct("z")
    tokens_grad = (grad_middle + grad_norm_one).reshape(seqs, piece, D)
    sum_value_rows = sum_values.result()
    sum_proj_input = jnp.concatenate([sum_query_key.result(), sum_value_rows[:, : HEADS * DV]], axis=1)
    found_extras = sum_value_rows[:, HEADS * DV :]

    decay_sums = jnp.pad(jnp.stack([grad_decay_log, grad_decay_bias]), ((0, 6), (0, 128 - HEADS)))
    decay_sums = everywhere(decay_sums)
    feed_rows = sum_feed.result()
    return (
        layer_out.reshape(seqs, piece, D),
        tokens_grad,
        sum_gain.result().reshape(own),
        sum_proj_input,
        found_extras[:, 2 * HEADS : 2 * HEADS + 16].reshape(-1, CONV),
        found_extras[:, : 2 * HEADS],
        sum_outgate.result(),
        found_extras[: gain_heads.shape[0], 2 * HEADS + 17],
        sum_output.result(),
        found_extras[:, 2 * HEADS + 16],
        feed_rows[:, :hidden_units],
        feed_rows[:, hidden_units:],
        sum_down.result(),
        decay_sums[0, :HEADS],
        decay_sums[1, :HEADS],
    )


def solution(mesh):
    dp, seq = mesh.shape["dp"], mesh.shape["seq"]
    side = math.isqrt(seq)
    side = side if side * side == seq else 1
    fine = jax.sharding.Mesh(mesh.devices.reshape(dp // 2, 2, seq // side, side), ALL)
    row, vector, split = P(("z", "c"), SEQ, None), P(ALL), P(ALL, None)
    in_specs = (row, row, vector, split, split, split, split, vector, split, vector, split, split, split, P(), P())
    out_specs = (row, row, vector, split, split, split, split, vector, split, vector, split, split, split, P(), P())
    return jax.shard_map(shards, mesh=fine, in_specs=in_specs, out_specs=out_specs, check_vma=False)
```
